512 devices in a mesh: runs: 64 (over z_lo, y, core), terms: 8 (over z_hi, x).
Axes of the slice: x: 4, y: 8, z: 8 (z_hi: 2, z_lo: 4; z = z_hi * 4 + z_lo), core: 2. Of those that a mesh axis runs over, the one named last changes fastest.
Arguments:
- design: bfloat16 [16384, 53248], P('runs', 'terms'), may hold values from -6 to 6
- responses: float32 [8, 16384], P(None, 'runs'), may hold values from -6 to 6
- picks: int32 [2, 256], replicated, may hold values from 0 to 53247, as said below
Outputs:
- residual: float32 [8, 16384], P(None, 'runs')
- correlations: float32 [8, 53248], P(None, 'terms')
The draws below stay inside these ranges and needn't reach their ends.
Inputs may be any that keep to these rules, and one draw needn't show every extreme that they name: `picks`: all 2 times 256 entries are distinct terms.
All inputs are finite; a program needn't handle non-finite values.
Results may differ from the reference program's by a relative error of at most 0.003.
Values may be sent and summed in bfloat16 or wider, within the bound.
No kernel may reach another device: no remote copies, remote signals or barrier semaphores. Data moves between devices by JAX's collectives and lax.ppermute only.
A program may use at most 64 MiB of HBM per device.

```python
import jax
import jax.numpy as jnp
from jax import lax

RESP = 8
SEL = 256
STEPS = 2
RUNS = 16384
TERMS = 53248


def draw_picks(key, part):
    key = jax.random.fold_in(key, 7)
    order = jax.random.permutation(key, TERMS)
    return order[:STEPS * SEL].reshape(STEPS, SEL).astype(jnp.int32)


def steps_of(own_key, shape, pieces, least, top_value):
    def one(position, shards_of):
        steps = jax.random.uniform(jax.random.fold_in(jax.random.fold_in(own_key, 6), position), (shards_of,), jnp.float32, least / len(pieces), top_value / len(pieces))
        return jnp.repeat(jnp.exp(steps), shape[position] // shards_of).reshape((-1,) + (1,) * (len(shape) - position - 1))

    loudness = one(*pieces[0])
    for cut in pieces[1:]:
        loudness = loudness * one(*cut)
    return loudness


def normal_values(stream_key, shape, width, bound, cuts=(), held_as=jnp.bfloat16):
    result = width * jax.random.normal(stream_key, shape, jnp.float32)
    if cuts:
        result = result * steps_of(stream_key, shape, cuts, -0.22, 0.18)
    return jnp.clip(result, -bound, bound).astype(held_as)


def setup_inputs(seed: int = 0) -> dict:
    keys = jax.random.split(jax.random.key(seed), 4)
    return {
        "design": normal_values(keys[0], (RUNS, TERMS), 1.0, 6.0, ((0, 64), (1, 8))),
        "responses": normal_values(keys[1], (RESP, RUNS), 1.0, 6.0, ((1, 64),), jnp.float32),
        "picks": draw_picks(jax.random.fold_in(keys[3], 71), 0),
    }


def reference(design, responses, picks):
    high = lax.Precision.HIGHEST
    residual = responses
    basis = None
    for step in range(STEPS):
        block = jnp.take(design, picks[step], axis=1).T.astype(jnp.float32)
        if basis is not None:
            proj = jnp.dot(basis, block.T, precision=high)
            block = block - jnp.dot(proj.T, basis, precision=high)
        gram = jnp.dot(block, block.T, precision=high)
        lower = jnp.linalg.cholesky(gram)
        newq = jax.scipy.linalg.solve_triangular(lower, block, lower=True)
        coef = jnp.dot(residual, newq.T, precision=high)
        residual = residual - jnp.dot(coef, newq, precision=high)
        basis = newq if basis is None else jnp.concatenate([basis, newq], axis=0)
    rounded = residual.astype(jnp.bfloat16)
    scale_factor = jnp.float32(RUNS) ** (-0.5)
    correlations = jnp.dot(rounded.astype(jnp.float32), design.astype(jnp.float32), preferred_element_type=jnp.float32) * scale_factor
    return (residual, correlations)
```

```python
import jax
import jax.numpy as jnp
from jax import lax
from jax.sharding import PartitionSpec as P

LANES = 128


def exchange(pieces, axis):
    return lax.all_to_all(pieces, axis, 0, 0)


def share(piece, axis):
    count = lax.axis_size(axis)
    return exchange(jnp.broadcast_to(piece[None], (count, *piece.shape)), axis)


def fetch_columns(design, indices):
    local_terms = design.shape[1]
    devices = lax.axis_size("terms")
    count = indices.shape[0]
    offset = lax.axis_index("terms") * local_terms
    positions = lax.broadcasted_iota(jnp.int32, (count, local_terms), 1)
    selector = (positions == (indices - offset)[:, None]).astype(jnp.bfloat16)
    partial_cols = lax.dot_general(
        selector, design, (((1,), (1,)), ((), ())), preferred_element_type=jnp.float32
    ).astype(jnp.bfloat16)
    pieces = exchange(partial_cols.reshape(devices, count // devices, -1), "terms")
    own = jnp.sum(pieces.astype(jnp.float32), axis=0).astype(jnp.bfloat16)
    return own, share(own, "terms").reshape(count, -1)


def local(design, responses, picks):
    high = lax.Precision.HIGHEST
    run_devices = lax.axis_size("runs")
    resp, local_rows = responses.shape
    indices = picks.reshape(-1)
    count = indices.shape[0]
    own, basis = fetch_columns(design, indices)
    basis32 = basis.astype(jnp.float32)
    gram_rows = lax.dot_general(
        own, basis, (((1,), (1,)), ((), ())), preferred_element_type=jnp.float32
    )
    inner_rows = lax.dot_general(
        own.astype(jnp.float32), responses, (((1,), (1,)), ((), ())), precision=high
    )
    rows = jnp.concatenate([gram_rows, inner_rows], axis=1)
    rows = jnp.pad(rows, ((0, 0), (0, -rows.shape[1] % LANES)))
    per = rows.shape[0] // run_devices
    summed = jnp.sum(exchange(rows.reshape(run_devices, per, -1), "runs"), axis=0)
    block = share(summed, "runs").reshape(rows.shape)
    system = share(block, "terms").reshape(count, -1)
    gram, inner = system[:, :count], system[:, count : count + resp]
    lower = jnp.linalg.cholesky(gram)
    half = jax.scipy.linalg.solve_triangular(lower, inner, lower=True)
    coef = jax.scipy.linalg.solve_triangular(lower, half, lower=True, trans=1).T
    residual = responses - jnp.dot(coef, basis32, precision=high)
    rounded = residual.astype(jnp.bfloat16)
    scale_factor = jnp.float32(local_rows * run_devices) ** (-0.5)
    partial_corr = jnp.dot(rounded, design, preferred_element_type=jnp.float32) * scale_factor
    tiles = partial_corr.shape[1] // LANES
    pieces = partial_corr.reshape(resp, tiles, LANES).transpose(1, 0, 2)
    pieces = jnp.pad(pieces, ((0, run_devices - tiles), (0, 0), (0, 0)))
    total = jnp.sum(exchange(pieces, "runs"), axis=0)
    gathered = share(total, "runs")[:tiles]
    correlations = gathered.transpose(1, 0, 2).reshape(resp, -1)
    return (residual, correlations)


def solution(mesh):
    placed = (P("runs", "terms"), P(None, "runs"), P())
    return jax.shard_map(
        local,
        mesh=mesh,
        in_specs=placed,
        out_specs=(P(None, "runs"), P(None, "terms")),
        check_vma=False,
    )
```

```python
import functools

import jax
import jax.numpy as jnp
from jax import lax
from jax.experimental import pallas as pl
from jax.experimental.pallas import tpu as pltpu
from jax.sharding import PartitionSpec as P

LANES = 128
SUB = 8
BLOCK = 128
HIGH = lax.Precision.HIGHEST


def exchange(pieces, axis):
    return lax.all_to_all(pieces, axis, 0, 0)


def share(piece, axis):
    count = lax.axis_size(axis)
    return exchange(jnp.broadcast_to(piece[None], (count, *piece.shape)), axis)


def fetch_columns(design, indices):
    local_terms = design.shape[1]
    devices = lax.axis_size("terms")
    count = indices.shape[0]
    offset = lax.axis_index("terms") * local_terms
    positions = lax.broadcasted_iota(jnp.int32, (count, local_terms), 1)
    selector = (positions == (indices - offset)[:, None]).astype(jnp.bfloat16)
    partial_cols = lax.dot_general(
        selector, design, (((1,), (1,)), ((), ())), preferred_element_type=jnp.float32
    ).astype(jnp.bfloat16)
    pieces = exchange(partial_cols.reshape(devices, count // devices, -1), "terms")
    own = jnp.sum(pieces.astype(jnp.float32), axis=0).astype(jnp.bfloat16)
    return own, share(own, "terms").reshape(count, -1)


def spread(piece):
    return jnp.broadcast_to(piece, (SUB, LANES))


def dot(left, right):
    return jnp.dot(left, right, precision=HIGH, preferred_element_type=jnp.float32)


def invert_small(columns, sub):
    for i in range(SUB):
        pivot = 1.0 / spread(columns[i][i : i + 1, :])
        column, here = columns[i], sub == i
        after = []
        for j in range(SUB):
            if j == i:
                after.append(jnp.where(here, pivot, -column * pivot))
            else:
                factor = spread(columns[j][i : i + 1, :]) * pivot
                after.append(jnp.where(here, factor, columns[j] - column * factor))
        columns = after
    return columns


def invert_block(groups):
    lane = lax.broadcasted_iota(jnp.int32, (SUB, LANES), 1)
    sub = lax.broadcasted_iota(jnp.int32, (SUB, LANES), 0)
    groups = list(groups)
    count = len(groups)
    for k in range(count):
        first = SUB * k
        mine = groups[k]
        small = invert_small(
            [spread(mine[:, first + j : first + j + 1]) for j in range(SUB)], sub
        )
        inside = (lane >= first) & (lane < first + SUB)
        unit = jnp.where(lane - first == sub, 1.0, 0.0)
        mine = jnp.where(inside, unit, mine)
        top = small[0] * spread(mine[0:1, :])
        for j in range(1, SUB):
            top = top + small[j] * spread(mine[j : j + 1, :])
        rows = [spread(top[j : j + 1, :]) for j in range(SUB)]
        for step in range(1, count):
            g = (k + step) % count
            new = jnp.where(inside, 0.0, groups[g])
            for j in range(SUB):
                new = new - spread(groups[g][:, first + j : first + j + 1]) * rows[j]
            groups[g] = new
        groups[k] = top
    return groups


def finish_kernel(
    scale, system, responses, basis, design, residual, pieces, work, inverse, held, sem
):
    count = basis.shape[0]
    resp = responses.shape[0]
    blocks = count // BLOCK
    copy = pltpu.make_async_copy(design, held, sem)
    copy.start()
    work[...] = system[...]

    def eliminate(k):
        start, stop = k * BLOCK, (k + 1) * BLOCK
        lead = dot(inverse[...], work[start:stop, stop:])
        work[:, stop:] = work[:, stop:] - dot(work[:, start:stop], lead)
        work[start:stop, stop:] = lead

    def step(k, carry):
        start = pl.multiple_of(k * BLOCK, BLOCK)
        groups = [
            work[pl.ds(pl.multiple_of(start + SUB * g, SUB), SUB), pl.ds(start, BLOCK)]
            for g in range(BLOCK // SUB)
        ]
        for g, group in enumerate(invert_block(groups)):
            inverse[SUB * g : SUB * (g + 1), :] = group
        for known in range(blocks):
            pl.when(k == known)(functools.partial(eliminate, known))
        return carry

    lax.fori_loop(0, blocks, step, 0)
    fitted = lax.dot_general(
        work[:, count : count + LANES],
        basis[...].astype(jnp.float32),
        (((0,), (0,)), ((), ())),
        precision=HIGH,
        preferred_element_type=jnp.float32,
    )
    left = responses[...] - fitted[:resp, :]
    residual[...] = left
    rounded = left.astype(jnp.bfloat16)
    copy.wait()
    tiles = held.shape[1] // LANES
    for tile in range(0, tiles, 2):
        part = held[:, tile * LANES : (tile + 2) * LANES]
        both = jnp.dot(rounded, part, preferred_element_type=jnp.float32) * scale
        pieces[tile] = both[:, :LANES]
        pieces[tile + 1] = both[:, LANES:]
    pieces[tiles:] = jnp.zeros((pieces.shape[0] - tiles, resp, LANES), jnp.float32)


def finish(system, responses, basis, design, pieces, scale):
    resp, rows = responses.shape
    whole = pl.BlockSpec(memory_space=pltpu.VMEM)
    return pl.pallas_call(
        functools.partial(finish_kernel, scale),
        out_shape=(
            jax.ShapeDtypeStruct((resp, rows), jnp.float32),
            jax.ShapeDtypeStruct((pieces, resp, LANES), jnp.float32),
        ),
        in_specs=[whole, whole, whole, pl.BlockSpec(memory_space=pl.ANY)],
        out_specs=(whole, whole),
        scratch_shapes=[
            pltpu.VMEM(system.shape, jnp.float32),
            pltpu.VMEM((BLOCK, BLOCK), jnp.float32),
            pltpu.VMEM(design.shape, design.dtype),
            pltpu.SemaphoreType.DMA,
        ],
        compiler_params=pltpu.CompilerParams(vmem_limit_bytes=32 * 2**20),
        name="finish",
    )(system, responses, basis, design)


def local(design, responses, picks):
    run_devices = lax.axis_size("runs")
    resp, local_rows = responses.shape
    indices = picks.reshape(-1)
    count = indices.shape[0]
    own, basis = fetch_columns(design, indices)
    gram_rows = lax.dot_general(
        own, basis, (((1,), (1,)), ((), ())), preferred_element_type=jnp.float32
    )
    inner_rows = lax.dot_general(
        own.astype(jnp.float32), responses, (((1,), (1,)), ((), ())), precision=HIGH
    )
    rows = jnp.concatenate([gram_rows, inner_rows], axis=1)
    rows = jnp.pad(rows, ((0, 0), (0, -rows.shape[1] % LANES)))
    per = rows.shape[0] // run_devices
    summed = jnp.sum(exchange(rows.reshape(run_devices, per, -1), "runs"), axis=0)
    block = share(summed, "runs").reshape(rows.shape)
    system = share(block, "terms").reshape(count, -1)
    scale = float(local_rows * run_devices) ** -0.5
    residual, pieces = finish(system, responses, basis, design, run_devices, scale)
    total = jnp.sum(exchange(pieces, "runs"), axis=0)
    tiles = design.shape[1] // LANES
    gathered = share(total, "runs")[:tiles]
    correlations = gathered.transpose(1, 0, 2).reshape(resp, -1)
    return (residual, correlations)


def solution(mesh):
    placed = (P("runs", "terms"), P(None, "runs"), P())
    return jax.shard_map(
        local,
        mesh=mesh,
        in_specs=placed,
        out_specs=(P(None, "runs"), P(None, "terms")),
        check_vma=False,
    )
```

```python
import functools

import jax
import jax.numpy as jnp
from jax import lax
from jax.experimental import pallas as pl
from jax.experimental.pallas import tpu as pltpu
from jax.sharding import PartitionSpec as P

LANES = 128
SUB = 8
BLOCK = 128
SLOTS = 96
CHUNKS = 4
HIGH = lax.Precision.HIGHEST
F32 = jnp.float32
BF16 = jnp.bfloat16


def call(kernel, name, out_shape, in_specs, out_specs, scratch=(), **more):
    return pl.pallas_call(
        kernel,
        out_shape=out_shape,
        in_specs=in_specs,
        out_specs=out_specs,
        scratch_shapes=scratch,
        compiler_params=pltpu.CompilerParams(vmem_limit_bytes=32 * 2**20),
        name=name,
        **more,
    )


WHOLE = pl.BlockSpec(memory_space=pltpu.VMEM)
SCALAR = pl.BlockSpec(memory_space=pltpu.SMEM)


def exchange(pieces, axis, groups=None):
    return lax.all_to_all(pieces, axis, 0, 0, axis_index_groups=groups)


def owners(picks, devices, local_terms):
    count = picks.shape[1]
    first = lax.broadcasted_iota(jnp.int32, (devices, count), 0) * local_terms
    owned = ((picks >= first) & (picks < first + local_terms)).astype(F32)
    before = lax.broadcasted_iota(jnp.int32, (count, count), 0)
    after = lax.broadcasted_iota(jnp.int32, (count, count), 1)
    rank = jnp.dot(
        owned.astype(BF16),
        (before < after).astype(F32).astype(BF16),
        preferred_element_type=F32,
    )
    return owned, rank


def pack_kernel(local_terms, place, picks, design, packed, most, where, total):
    step = pl.program_id(0)
    devices = packed.shape[0]
    chunk = design.shape[1]

    @pl.when(step == 0)
    def _():
        owned, rank = owners(picks[...], devices, local_terms)
        counts = jnp.sum(owned, axis=1, keepdims=True)
        most[0] = jnp.max(counts).astype(jnp.int32)
        me = lax.broadcasted_iota(jnp.int32, owned.shape, 0) == place[0]
        mine = jnp.where(me, owned, 0.0)
        slot = jnp.sum(mine * rank, axis=0, keepdims=True)
        slot = slot - (place[1] * SLOTS).astype(F32)
        slot = jnp.where(jnp.sum(mine, axis=0, keepdims=True) > 0.0, slot, -1.0)
        slots = lax.broadcasted_iota(jnp.int32, (SLOTS, slot.shape[1]), 0).astype(F32)
        inner = (picks[...] - place[0] * local_terms + 1).astype(F32)
        held = jnp.where(slots == slot, inner, 0.0)
        where[...] = jnp.sum(held, axis=1, keepdims=True).astype(jnp.int32) - 1
        total[...] = jnp.zeros_like(total)

    columns = lax.broadcasted_iota(jnp.int32, (SLOTS, chunk), 1) + step * chunk
    chosen = (columns == where[...]).astype(F32).astype(BF16)
    total[...] += lax.dot_general(
        chosen, design[...], (((1,), (1,)), ((), ())), preferred_element_type=F32
    )

    @pl.when(step == CHUNKS - 1)
    def _():
        value = total[...].astype(BF16)
        for partner in range(devices):
            packed[partner] = value


def pack(place, picks, design, devices):
    rows, local_terms = design.shape
    chunk = local_terms // CHUNKS
    return call(
        functools.partial(pack_kernel, local_terms),
        "pack",
        (
            jax.ShapeDtypeStruct((devices, SLOTS, rows), BF16),
            jax.ShapeDtypeStruct((1,), jnp.int32),
        ),
        [SCALAR, WHOLE, pl.BlockSpec((rows, chunk), lambda step: (0, step))],
        (WHOLE, SCALAR),
        [pltpu.VMEM((SLOTS, 1), jnp.int32), pltpu.VMEM((SLOTS, rows), F32)],
        grid=(CHUNKS,),
    )(place, picks, design)


def upper_blocks(blocks):
    return [(i, j) for i in range(blocks) for j in range(i, blocks)]


def gram_kernel(local_terms, devices, place, picks, slots, responses, *refs):
    *prior, basis, keep, send, packed = refs
    owned, rank = owners(picks[...], devices, local_terms)
    first = lax.broadcasted_iota(jnp.int32, owned.shape, 0).astype(F32) * SLOTS
    slot = jnp.sum(owned * rank, axis=0, keepdims=True)
    slot = slot - (place[1] * SLOTS).astype(F32)
    target = slot + jnp.sum(owned * first, axis=0, keepdims=True)
    target = jnp.where((slot >= 0.0) & (slot < SLOTS), target, -1.0)
    count = picks.shape[1]
    lines = lax.broadcasted_iota(jnp.int32, (devices * SLOTS, count), 0).astype(F32)
    moved = (lines == target).astype(F32).astype(BF16)
    columns = lax.dot_general(
        moved, slots[...], (((0,), (0,)), ((), ())), preferred_element_type=F32
    )
    if prior:
        columns = columns + prior[0][...].astype(F32)
    columns = columns.astype(BF16)
    basis[...] = columns
    blocks = count // BLOCK
    row = 0
    for i in range(blocks):
        strip = lax.dot_general(
            columns[i * BLOCK : (i + 1) * BLOCK],
            columns[i * BLOCK :],
            (((1,), (1,)), ((), ())),
            preferred_element_type=F32,
        )
        for j in range(blocks - i):
            packed[row : row + BLOCK, :] = strip[:, j * BLOCK : (j + 1) * BLOCK]
            row += BLOCK
    resp = responses.shape[0]
    rest, parts = responses[...], []
    for _ in range(3):
        part = rest.astype(BF16).astype(F32)
        parts.append(part)
        rest = rest - part
    inner = lax.dot_general(
        jnp.concatenate(parts, axis=0).astype(BF16),
        columns,
        (((1,), (1,)), ((), ())),
        preferred_element_type=F32,
    )
    inner = inner[2 * resp :] + inner[resp : 2 * resp] + inner[:resp]
    for j in range(blocks):
        packed[row : row + resp, :] = inner[:, j * BLOCK : (j + 1) * BLOCK]
        row += resp
    packed[row:, :] = jnp.zeros((packed.shape[0] - row, LANES), F32)
    half = keep.shape[0]
    core = place[2]
    keep[...] = packed[pl.ds(pl.multiple_of(core * half, SUB), half), :]
    send[...] = packed[pl.ds(pl.multiple_of((1 - core) * half, SUB), half), :]


def gram(place, picks, slots, responses, prior, local_terms, half):
    devices, _, rows = slots.shape
    count = picks.shape[1]
    operands = (place, picks, slots.reshape(-1, rows), responses, *prior)
    return call(
        functools.partial(gram_kernel, local_terms, devices),
        "gram",
        (
            jax.ShapeDtypeStruct((count, rows), BF16),
            jax.ShapeDtypeStruct((half, LANES), F32),
            jax.ShapeDtypeStruct((half, LANES), F32),
        ),
        [SCALAR] + [WHOLE] * (len(operands) - 1),
        (WHOLE, WHOLE, WHOLE),
        [pltpu.VMEM((2 * half, LANES), F32)],
    )(*operands)


def spread(piece):
    return jnp.broadcast_to(piece, (SUB, LANES))


def dot(left, right):
    return jnp.dot(left, right, precision=HIGH, preferred_element_type=F32)


def dot_first(left, right):
    return lax.dot_general(
        left,
        right,
        (((0,), (0,)), ((), ())),
        precision=HIGH,
        preferred_element_type=F32,
    )


def invert_small(columns, sub):
    for i in range(SUB):
        pivot = 1.0 / spread(columns[i][i : i + 1, :])
        column, here = columns[i], sub == i
        after = []
        for j in range(SUB):
            if j == i:
                after.append(jnp.where(here, pivot, -column * pivot))
            else:
                factor = spread(columns[j][i : i + 1, :]) * pivot
                after.append(jnp.where(here, factor, columns[j] - column * factor))
        columns = after
    return columns


def invert_block(groups):
    lane = lax.broadcasted_iota(jnp.int32, (SUB, LANES), 1)
    sub = lax.broadcasted_iota(jnp.int32, (SUB, LANES), 0)
    groups = list(groups)
    count = len(groups)
    for k in range(count):
        first = SUB * k
        mine = groups[k]
        small = invert_small(
            [spread(mine[:, first + j : first + j + 1]) for j in range(SUB)], sub
        )
        inside = (lane >= first) & (lane < first + SUB)
        unit = jnp.where(lane - first == sub, 1.0, 0.0)
        mine = jnp.where(inside, unit, mine)
        top = small[0] * spread(mine[0:1, :])
        for j in range(1, SUB):
            top = top + small[j] * spread(mine[j : j + 1, :])
        rows = [spread(top[j : j + 1, :]) for j in range(SUB)]
        for step in range(1, count):
            g = (k + step) % count
            new = jnp.where(inside, 0.0, groups[g])
            for j in range(SUB):
                new = new - spread(groups[g][:, first + j : first + j + 1]) * rows[j]
            groups[g] = new
        groups[k] = top
    return groups


def finish_kernel(scale, place, *refs):
    mine, other, responses, basis, design, residual, pieces = refs[:7]
    packed, work, inverse, coef = refs[7:]
    half = mine.shape[0]
    count = basis.shape[0]
    resp = responses.shape[0]
    blocks = count // BLOCK
    core = place[2]
    packed[pl.ds(pl.multiple_of(core * half, SUB), half), :] = mine[...]
    packed[pl.ds(pl.multiple_of((1 - core) * half, SUB), half), :] = other[...]
    row = 0
    for i, j in upper_blocks(blocks):
        work[i * BLOCK : (i + 1) * BLOCK, j * BLOCK : (j + 1) * BLOCK] = packed[
            row : row + BLOCK, :
        ]
        row += BLOCK
    for i in range(blocks):
        inner = packed[row : row + resp, :]
        tall = jnp.concatenate([inner, jnp.zeros((BLOCK - resp, BLOCK), F32)], axis=0)
        work[i * BLOCK : (i + 1) * BLOCK, count:] = tall.T
        row += resp

    def eliminate(k):
        start, stop = k * BLOCK, (k + 1) * BLOCK
        right = work[start:stop, stop:]
        lead = dot(inverse[...], right)
        if stop < count:
            work[stop:, stop:] = work[stop:, stop:] - dot_first(
                right[:, : count - stop], lead
            )
        work[start:stop, stop:] = lead

    def step(k, carry):
        start = pl.multiple_of(k * BLOCK, BLOCK)
        groups = [
            work[pl.ds(pl.multiple_of(start + SUB * g, SUB), SUB), pl.ds(start, BLOCK)]
            for g in range(BLOCK // SUB)
        ]
        for g, group in enumerate(invert_block(groups)):
            inverse[SUB * g : SUB * (g + 1), :] = group
        for known in range(blocks):
            pl.when(k == known)(functools.partial(eliminate, known))
        return carry

    lax.fori_loop(0, blocks, step, 0)
    coef[count - BLOCK :, :] = work[count - BLOCK :, count:]
    for k in reversed(range(blocks - 1)):
        start, stop = k * BLOCK, (k + 1) * BLOCK
        coef[start:stop, :] = work[start:stop, count:] - dot(
            work[start:stop, stop:count], coef[stop:, :]
        )
    fitted = dot_first(coef[...], basis[...].astype(F32))
    left = responses[...] - fitted[:resp, :]
    residual[...] = left
    rounded = left.astype(BF16)
    tiles = design.shape[1] // LANES
    for tile in range(0, tiles, 2):
        part = design[:, tile * LANES : (tile + 2) * LANES]
        both = jnp.dot(rounded, part, preferred_element_type=F32) * scale
        pieces[tile] = both[:, :LANES]
        pieces[tile + 1] = both[:, LANES:]
    pieces[tiles:] = jnp.zeros((pieces.shape[0] - tiles, resp, LANES), F32)


def finish(place, mine, other, responses, basis, design, pieces, scale):
    resp, rows = responses.shape
    count = basis.shape[0]
    return call(
        functools.partial(finish_kernel, scale),
        "finish",
        (
            jax.ShapeDtypeStruct((resp, rows), F32),
            jax.ShapeDtypeStruct((pieces, resp, LANES), F32),
        ),
        [SCALAR] + [WHOLE] * 5,
        (WHOLE, WHOLE),
        [
            pltpu.VMEM((2 * mine.shape[0], LANES), F32),
            pltpu.VMEM((count, count + LANES), F32),
            pltpu.VMEM((BLOCK, BLOCK), F32),
            pltpu.VMEM((count, LANES), F32),
        ],
    )(place, mine, other, responses, basis, design)


def summed_everywhere(pieces, axis, groups=None):
    total = jnp.sum(exchange(pieces, axis, groups), axis=0)
    return exchange(jnp.broadcast_to(total[None], pieces.shape), axis, groups)


def local(design, responses, picks):
    run_devices, term_devices = lax.axis_size("runs"), lax.axis_size("terms")
    resp, local_rows = responses.shape
    local_terms = design.shape[1]
    chips = run_devices // 2
    core = lax.axis_index("runs") % 2
    place = [lax.axis_index("terms"), 0, core]
    picks = picks.reshape(1, -1)
    count = picks.shape[1]

    blocks = count // BLOCK
    lines = len(upper_blocks(blocks)) * BLOCK + blocks * resp
    lines += -lines % (run_devices * SUB)
    half = lines // 2

    def fetch(turn):
        at = jnp.stack([jnp.int32(v) for v in (place[0], turn, place[2])])
        packed, most = pack(at, picks, design, term_devices)
        return at, exchange(packed, "terms"), most

    at, slots, most = fetch(0)
    state = gram(at, picks, slots, responses, (), local_terms, half)

    def another(carry):
        turn, basis, _, _ = carry
        where, more, _ = fetch(turn)
        return turn + 1, *gram(
            where, picks, more, responses, (basis,), local_terms, half
        )

    _, basis, keep, send = lax.while_loop(
        lambda carry: carry[0] * SLOTS < most[0], another, (jnp.int32(1), *state)
    )

    swap = [(i, i ^ 1) for i in range(run_devices)]
    sides = [list(range(side, run_devices, 2)) for side in range(2)]
    part = keep + lax.ppermute(send, "runs", swap)
    mine = summed_everywhere(part.reshape(chips, -1, LANES), "runs", sides)
    mine = mine.reshape(half, LANES)
    other = lax.ppermute(mine, "runs", swap)

    scale = float(local_rows * run_devices) ** -0.5
    residual, pieces = finish(
        at, mine, other, responses, basis, design, run_devices, scale
    )
    gathered = summed_everywhere(pieces, "runs")[: local_terms // LANES]
    correlations = gathered.transpose(1, 0, 2).reshape(resp, -1)
    return (residual, correlations)


def solution(mesh):
    placed = (P("runs", "terms"), P(None, "runs"), P())
    return jax.shard_map(
        local,
        mesh=mesh,
        in_specs=placed,
        out_specs=(P(None, "runs"), P(None, "terms")),
        check_vma=False,
    )
```

```python
import functools

import jax
import jax.numpy as jnp
from jax import lax
from jax.experimental import pallas as pl
from jax.experimental.pallas import tpu as pltpu
from jax.sharding import PartitionSpec as P

LANES = 128
SUB = 8
BLOCK = 128
SLOTS = 96
CHUNKS = 4
HALVES = (
    ((0, 128, 0, 512), (128, 256, 128, 256), (128, 192, 256, 384)),
    (
        (0, 128, 0, 128),
        (192, 256, 256, 384),
        (128, 256, 384, 512),
        (256, 384, 256, 512),
        (384, 512, 384, 512),
    ),
)
HIGH = lax.Precision.HIGHEST
F32 = jnp.float32
BF16 = jnp.bfloat16


def call(kernel, name, out_shape, in_specs, out_specs, scratch=(), **more):
    return pl.pallas_call(
        kernel,
        out_shape=out_shape,
        in_specs=in_specs,
        out_specs=out_specs,
        scratch_shapes=scratch,
        compiler_params=pltpu.CompilerParams(vmem_limit_bytes=32 * 2**20),
        name=name,
        **more,
    )


WHOLE = pl.BlockSpec(memory_space=pltpu.VMEM)
SCALAR = pl.BlockSpec(memory_space=pltpu.SMEM)


def exchange(pieces, axis, groups=None):
    return lax.all_to_all(pieces, axis, 0, 0, axis_index_groups=groups)


def as_line(picks):
    return jnp.concatenate([picks[i : i + 1, :] for i in range(picks.shape[0])], axis=1)


def owners(picks, devices, local_terms):
    count = picks.shape[1]
    first = lax.broadcasted_iota(jnp.int32, (devices, count), 0) * local_terms
    owned = ((picks >= first) & (picks < first + local_terms)).astype(F32)
    before = lax.broadcasted_iota(jnp.int32, (count, count), 0)
    after = lax.broadcasted_iota(jnp.int32, (count, count), 1)
    rank = jnp.dot(
        owned.astype(BF16),
        (before < after).astype(F32).astype(BF16),
        preferred_element_type=F32,
    )
    return owned, rank


def pack_kernel(place, picks, design, packed, most, held, where, sems):
    devices = packed.shape[0]
    local_terms = design.shape[1]
    chunk = local_terms // CHUNKS

    def part(step):
        columns = pl.ds(step * chunk, chunk)
        return pltpu.make_async_copy(
            design.at[:, columns], held.at[:, columns], sems.at[step]
        )

    for step in range(CHUNKS):
        part(step).start()
    line = as_line(picks)
    owned, rank = owners(line, devices, local_terms)
    counts = jnp.sum(owned, axis=1, keepdims=True)
    most[0] = jnp.max(counts).astype(jnp.int32)
    me = lax.broadcasted_iota(jnp.int32, owned.shape, 0) == place[0]
    mine = jnp.where(me, owned, 0.0)
    slot = jnp.sum(mine * rank, axis=0, keepdims=True)
    slot = slot - (place[1] * SLOTS).astype(F32)
    slot = jnp.where(jnp.sum(mine, axis=0, keepdims=True) > 0.0, slot, -1.0)
    slots = lax.broadcasted_iota(jnp.int32, (SLOTS, slot.shape[1]), 0).astype(F32)
    inner = (line - place[0] * local_terms + 1).astype(F32)
    inner = jnp.where(slots == slot, inner, 0.0)
    where[...] = jnp.sum(inner, axis=1, keepdims=True).astype(jnp.int32) - 1
    total = jnp.zeros((SLOTS, design.shape[0]), F32)
    for step in range(CHUNKS):
        columns = lax.broadcasted_iota(jnp.int32, (SLOTS, chunk), 1) + step * chunk
        chosen = (columns == where[...]).astype(F32).astype(BF16)
        part(step).wait()
        total = total + lax.dot_general(
            chosen,
            held[:, step * chunk : (step + 1) * chunk],
            (((1,), (1,)), ((), ())),
            preferred_element_type=F32,
        )
    value = total.astype(BF16)
    for partner in range(devices):
        packed[partner] = value


def pack(place, picks, design, devices):
    rows = design.shape[0]
    return call(
        pack_kernel,
        "pack",
        (
            jax.ShapeDtypeStruct((devices, SLOTS, rows), BF16),
            jax.ShapeDtypeStruct((1,), jnp.int32),
        ),
        [SCALAR, WHOLE, pl.BlockSpec(memory_space=pltpu.HBM)],
        (WHOLE, SCALAR),
        [
            pltpu.VMEM(design.shape, design.dtype),
            pltpu.VMEM((SLOTS, 1), jnp.int32),
            pltpu.SemaphoreType.DMA((CHUNKS,)),
        ],
    )(place, picks, design)


def gram_kernel(local_terms, devices, has_prior, place, picks, slots, other, *refs):
    own = other.shape[0] != refs[-1].shape[0]
    prior = refs[0] if has_prior else None
    basis, sums = refs[-2:]
    owned, rank = owners(as_line(picks), devices, local_terms)
    first = lax.broadcasted_iota(jnp.int32, owned.shape, 0).astype(F32) * SLOTS
    slot = jnp.sum(owned * rank, axis=0, keepdims=True)
    slot = slot - (place[1] * SLOTS).astype(F32)
    target = slot + jnp.sum(owned * first, axis=0, keepdims=True)
    target = jnp.where((slot >= 0.0) & (slot < SLOTS), target, -1.0)
    count = target.shape[1]
    lines = lax.broadcasted_iota(jnp.int32, (devices * SLOTS, count), 0).astype(F32)
    moved = (lines == target).astype(F32).astype(BF16)
    columns = lax.dot_general(
        moved, slots[...], (((0,), (0,)), ((), ())), preferred_element_type=F32
    )
    if has_prior:
        columns = columns + prior[...].astype(F32)
    basis[...] = columns.astype(BF16)

    def fill(side):
        row = 0
        for top, bottom, start, stop in HALVES[side]:
            strip = lax.dot_general(
                basis[top:bottom],
                basis[start:stop],
                (((1,), (1,)), ((), ())),
                preferred_element_type=F32,
            )
            for j in range(0, stop - start, BLOCK):
                after = row + bottom - top
                piece = strip[:, j : j + BLOCK]
                sums[row:after, :] = piece if own else piece + other[row:after, :]
                row = after
        if not own:
            sums[row:, :] = other[row:, :]
            return
        resp = other.shape[0]
        rest, parts = other[...], []
        for _ in range(3):
            part = rest.astype(BF16).astype(F32)
            parts.append(part)
            rest = rest - part
        inner = lax.dot_general(
            jnp.concatenate(parts, axis=0).astype(BF16),
            basis[...],
            (((1,), (1,)), ((), ())),
            preferred_element_type=F32,
        )
        inner = inner[2 * resp :] + inner[resp : 2 * resp] + inner[:resp]
        for j in range(0, count, BLOCK):
            sums[row : row + resp, :] = inner[:, j : j + BLOCK]
            row += resp
        sums[row:, :] = jnp.zeros((sums.shape[0] - row, LANES), F32)

    for side in range(2):
        pl.when(place[2] == side)(functools.partial(fill, side))


def gram(place, picks, slots, other, local_terms, half, prior=None):
    devices, _, rows = slots.shape
    count = picks.size
    extra = () if prior is None else (prior,)
    operands = (place, picks, slots.reshape(-1, rows), other, *extra)
    return call(
        functools.partial(gram_kernel, local_terms, devices, prior is not None),
        "gram",
        (
            jax.ShapeDtypeStruct((count, rows), BF16),
            jax.ShapeDtypeStruct((half, LANES), F32),
        ),
        [SCALAR] + [WHOLE] * (len(operands) - 1),
        (WHOLE, WHOLE),
        cost_estimate=pl.CostEstimate(
            flops=2 * count * rows * (devices * SLOTS + count),
            bytes_accessed=2 * count * rows,
            transcendentals=0,
        ),
    )(*operands)


def total_kernel(pieces, totals):
    total = jnp.sum(pieces[...], axis=0)
    for piece in range(totals.shape[0]):
        totals[piece] = total


def totals(pieces):
    shape = jax.ShapeDtypeStruct(pieces.shape, pieces.dtype)
    return call(total_kernel, "totals", shape, [WHOLE], WHOLE)(pieces)


def spread(piece):
    return jnp.broadcast_to(piece, (SUB, LANES))


def dot(left, right):
    return jnp.dot(left, right, precision=HIGH, preferred_element_type=F32)


def dot_first(left, right):
    return lax.dot_general(
        left,
        right,
        (((0,), (0,)), ((), ())),
        precision=HIGH,
        preferred_element_type=F32,
    )


def across(group, lane):
    index = jnp.full((SUB, LANES), lane, jnp.int32)
    return jnp.take_along_axis(group, index, axis=1, mode="promise_in_bounds")


def invert_small(columns, sub):
    for i in range(SUB):
        pivot = 1.0 / spread(columns[i][i : i + 1, :])
        column, here = columns[i], sub == i
        after = []
        for j in range(SUB):
            if j == i:
                after.append(jnp.where(here, pivot, -column * pivot))
            else:
                factor = spread(columns[j][i : i + 1, :]) * pivot
                after.append(jnp.where(here, factor, columns[j] - column * factor))
        columns = after
    return columns


def invert_block(groups):
    lane = lax.broadcasted_iota(jnp.int32, (SUB, LANES), 1)
    sub = lax.broadcasted_iota(jnp.int32, (SUB, LANES), 0)
    groups = list(groups)
    count = len(groups)
    for k in range(count):
        first = SUB * k
        mine = groups[k]
        small = invert_small(
            [across(mine, first + j) for j in range(SUB)], sub
        )
        inside = (lane >= first) & (lane < first + SUB)
        unit = jnp.where(lane - first == sub, 1.0, 0.0)
        mine = jnp.where(inside, unit, mine)
        top = small[0] * spread(mine[0:1, :])
        for j in range(1, SUB):
            top = top + small[j] * spread(mine[j : j + 1, :])
        rows = [spread(top[j : j + 1, :]) for j in range(SUB)]
        for step in range(1, count):
            g = (k + step) % count
            new = jnp.where(inside, 0.0, groups[g])
            for j in range(SUB):
                new = new - across(groups[g], first + j) * rows[j]
            groups[g] = new
        groups[k] = top
    return groups


def groups_of(block):
    return [block[SUB * g : SUB * (g + 1), :] for g in range(BLOCK // SUB)]


def first_kernel(sums, inverse):
    for g, group in enumerate(invert_block(groups_of(sums[:BLOCK, :]))):
        inverse[SUB * g : SUB * (g + 1), :] = group


def first_inverse(sums):
    return call(
        first_kernel,
        "first_inverse",
        jax.ShapeDtypeStruct((BLOCK, BLOCK), F32),
        [WHOLE],
        WHOLE,
        cost_estimate=pl.CostEstimate(
            flops=2 * 10**9, bytes_accessed=10**5, transcendentals=0
        ),
    )(sums)


def finish_kernel(scale, place, *refs):
    mine, other, known_inverse, responses, basis, design, residual, pieces = refs[:8]
    packed, work, inverse, coef = refs[8:]
    half = mine.shape[0]
    count = basis.shape[0]
    resp = responses.shape[0]
    blocks = count // BLOCK
    core = place[2]
    packed[pl.ds(pl.multiple_of(core * half, SUB), half), :] = mine[...]
    packed[pl.ds(pl.multiple_of((1 - core) * half, SUB), half), :] = other[...]
    ends = []
    for side in range(2):
        row = side * half
        for top, bottom, start, stop in HALVES[side]:
            for j in range(start, stop, BLOCK):
                after = row + bottom - top
                work[top:bottom, j : j + BLOCK] = packed[row:after, :]
                row = after
        ends.append(row)
    for i in range(blocks):
        inner = [packed[end + i * resp : end + (i + 1) * resp, :] for end in ends]
        tall = [inner[0] + inner[1], jnp.zeros((BLOCK - resp, BLOCK), F32)]
        work[i * BLOCK : (i + 1) * BLOCK, count:] = jnp.concatenate(tall, axis=0).T

    def eliminate(k):
        start, stop = k * BLOCK, (k + 1) * BLOCK
        right = work[start:stop, stop:]
        lead = dot(inverse[...], right)
        if stop < count:
            work[stop:, stop:] = work[stop:, stop:] - dot_first(
                right[:, : count - stop], lead
            )
        work[start:stop, stop:] = lead

    def step(k, carry):
        start = pl.multiple_of(k * BLOCK, BLOCK)
        groups = [
            work[pl.ds(pl.multiple_of(start + SUB * g, SUB), SUB), pl.ds(start, BLOCK)]
            for g in range(BLOCK // SUB)
        ]
        for g, group in enumerate(invert_block(groups)):
            inverse[SUB * g : SUB * (g + 1), :] = group
        for known in range(1, blocks):
            pl.when(k == known)(functools.partial(eliminate, known))
        return carry

    inverse[...] = known_inverse[...]
    eliminate(0)
    lax.fori_loop(1, blocks, step, 0)
    coef[count - BLOCK :, :] = work[count - BLOCK :, count:]
    for k in reversed(range(blocks - 1)):
        start, stop = k * BLOCK, (k + 1) * BLOCK
        coef[start:stop, :] = work[start:stop, count:] - dot(
            work[start:stop, stop:count], coef[stop:, :]
        )
    fitted = dot_first(coef[...], basis[...].astype(F32))
    left = responses[...] - fitted[:resp, :]
    residual[...] = left
    rounded = left.astype(BF16)
    tiles = design.shape[1] // LANES
    for tile in range(0, tiles, 2):
        part = design[:, tile * LANES : (tile + 2) * LANES]
        both = jnp.dot(rounded, part, preferred_element_type=F32) * scale
        pieces[tile] = both[:, :LANES]
        pieces[tile + 1] = both[:, LANES:]
    pieces[tiles:] = jnp.zeros((pieces.shape[0] - tiles, resp, LANES), F32)


def finish(place, mine, other, inverse, responses, basis, design, pieces, scale):
    resp, rows = responses.shape
    count = basis.shape[0]
    return call(
        functools.partial(finish_kernel, scale),
        "finish",
        (
            jax.ShapeDtypeStruct((resp, rows), F32),
            jax.ShapeDtypeStruct((pieces, resp, LANES), F32),
        ),
        [SCALAR] + [WHOLE] * 6,
        (WHOLE, WHOLE),
        [
            pltpu.VMEM((2 * mine.shape[0], LANES), F32),
            pltpu.VMEM((count, count + LANES), F32),
            pltpu.VMEM((BLOCK, BLOCK), F32),
            pltpu.VMEM((count, LANES), F32),
        ],
    )(place, mine, other, inverse, responses, basis, design)


def summed_everywhere(pieces, axis, groups=None):
    return exchange(totals(exchange(pieces, axis, groups)), axis, groups)


def local(design, responses, picks):
    run_devices, term_devices = lax.axis_size("runs"), lax.axis_size("terms")
    resp, local_rows = responses.shape
    local_terms = design.shape[1]
    chips = run_devices // 2
    core = lax.axis_index("runs") % 2
    swap = [(i, i ^ 1) for i in range(run_devices)]
    sides = [list(range(side, run_devices, 2)) for side in range(2)]
    count = picks.size
    half = (4 + 2) * BLOCK

    def fetch(turn):
        where = jnp.stack([lax.axis_index("terms"), jnp.int32(turn), core])
        packed, most = pack(where, picks, design, term_devices)
        return where, exchange(packed, "terms"), most

    def grams(where, slots, prior=(None, None)):
        partner_slots = lax.ppermute(slots, "runs", swap)
        basis, sums = gram(
            where, picks, slots, responses, local_terms, half, prior[0]
        )
        partner_basis, sums = gram(
            where, picks, partner_slots, sums, local_terms, half, prior[1]
        )
        return basis, partner_basis, sums

    at, slots, most = fetch(0)
    state = grams(at, slots)

    def another(carry):
        turn, basis, partner_basis, _ = carry
        where, more, _ = fetch(turn)
        return turn + 1, *grams(where, more, (basis, partner_basis))

    _, basis, _, sums = lax.while_loop(
        lambda carry: carry[0] * SLOTS < most[0], another, (jnp.int32(1), *state)
    )

    mine = summed_everywhere(sums.reshape(chips, -1, LANES), "runs", sides)
    mine = mine.reshape(half, LANES)
    other = lax.ppermute(mine, "runs", swap)
    inverse = first_inverse(mine)

    scale = float(local_rows * run_devices) ** -0.5
    residual, pieces = finish(
        at, mine, other, inverse, responses, basis, design, run_devices, scale
    )
    gathered = summed_everywhere(pieces, "runs")[: local_terms // LANES]
    correlations = gathered.transpose(1, 0, 2).reshape(resp, -1)
    return (residual, correlations)


def solution(mesh):
    placed = (P("runs", "terms"), P(None, "runs"), P())
    return jax.shard_map(
        local,
        mesh=mesh,
        in_specs=placed,
        out_specs=(P(None, "runs"), P(None, "terms")),
        check_vma=False,
    )
```

```python
import functools

import jax
import jax.numpy as jnp
from jax import lax
from jax.experimental import pallas as pl
from jax.experimental.pallas import tpu as pltpu
from jax.sharding import PartitionSpec as P

LANES = 128
SUB = 8
BLOCK = 128
SLOTS = 96
CHUNKS = 4
HALVES = (
    ((0, 128, 0, 512), (128, 256, 128, 256), (128, 192, 256, 384)),
    (
        (0, 128, 0, 128),
        (192, 256, 256, 384),
        (128, 256, 384, 512),
        (256, 384, 256, 512),
        (384, 512, 384, 512),
    ),
)
INNER = 704
HIGH = lax.Precision.HIGHEST
F32 = jnp.float32
BF16 = jnp.bfloat16


def call(kernel, name, out_shape, in_specs, out_specs, scratch=(), vmem=32, **more):
    return pl.pallas_call(
        kernel,
        out_shape=out_shape,
        in_specs=in_specs,
        out_specs=out_specs,
        scratch_shapes=scratch,
        compiler_params=pltpu.CompilerParams(vmem_limit_bytes=vmem * 2**20),
        name=name,
        **more,
    )


WHOLE = pl.BlockSpec(memory_space=pltpu.VMEM)
SCALAR = pl.BlockSpec(memory_space=pltpu.SMEM)


def exchange(pieces, axis, groups=None):
    return lax.all_to_all(pieces, axis, 0, 0, axis_index_groups=groups)


def as_line(picks):
    return jnp.concatenate([picks[i : i + 1, :] for i in range(picks.shape[0])], axis=1)


def owners(picks, devices, local_terms):
    count = picks.shape[1]
    first = lax.broadcasted_iota(jnp.int32, (devices, count), 0) * local_terms
    owned = ((picks >= first) & (picks < first + local_terms)).astype(F32)
    before = lax.broadcasted_iota(jnp.int32, (count, count), 0)
    after = lax.broadcasted_iota(jnp.int32, (count, count), 1)
    rank = jnp.dot(
        owned.astype(BF16),
        (before < after).astype(F32).astype(BF16),
        preferred_element_type=F32,
    )
    return owned, rank


def pack_kernel(place, picks, design, packed, most, held, where, sems):
    devices = packed.shape[0]
    local_terms = design.shape[1]
    chunk = local_terms // CHUNKS

    def part(step):
        columns = pl.ds(step * chunk, chunk)
        return pltpu.make_async_copy(
            design.at[:, columns], held.at[:, columns], sems.at[step]
        )

    for step in range(CHUNKS):
        part(step).start()
    line = as_line(picks)
    owned, rank = owners(line, devices, local_terms)
    counts = jnp.sum(owned, axis=1, keepdims=True)
    most[0] = jnp.max(counts).astype(jnp.int32)
    me = lax.broadcasted_iota(jnp.int32, owned.shape, 0) == place[0]
    mine = jnp.where(me, owned, 0.0)
    slot = jnp.sum(mine * rank, axis=0, keepdims=True)
    slot = slot - (place[1] * SLOTS).astype(F32)
    slot = jnp.where(jnp.sum(mine, axis=0, keepdims=True) > 0.0, slot, -1.0)
    slots = lax.broadcasted_iota(jnp.int32, (SLOTS, slot.shape[1]), 0).astype(F32)
    inner = (line - place[0] * local_terms + 1).astype(F32)
    inner = jnp.where(slots == slot, inner, 0.0)
    where[...] = jnp.sum(inner, axis=1, keepdims=True).astype(jnp.int32) - 1
    total = jnp.zeros((SLOTS, design.shape[0]), F32)
    for step in range(CHUNKS):
        columns = lax.broadcasted_iota(jnp.int32, (SLOTS, chunk), 1) + step * chunk
        chosen = (columns == where[...]).astype(F32).astype(BF16)
        part(step).wait()
        total = total + lax.dot_general(
            chosen,
            held[:, step * chunk : (step + 1) * chunk],
            (((1,), (1,)), ((), ())),
            preferred_element_type=F32,
        )
    value = total.astype(BF16)
    for partner in range(devices):
        packed[partner] = value


def pack(place, picks, design, devices):
    rows = design.shape[0]
    return call(
        pack_kernel,
        "pack",
        (
            jax.ShapeDtypeStruct((devices, SLOTS, rows), BF16),
            jax.ShapeDtypeStruct((1,), jnp.int32),
        ),
        [SCALAR, WHOLE, pl.BlockSpec(memory_space=pltpu.HBM)],
        (WHOLE, SCALAR),
        [
            pltpu.VMEM(design.shape, design.dtype),
            pltpu.VMEM((SLOTS, 1), jnp.int32),
            pltpu.SemaphoreType.DMA((CHUNKS,)),
        ],
        vmem=61,
    )(place, picks, design)


def gram_kernel(local_terms, devices, has_prior, place, picks, slots, other, *refs):
    own = other.shape[0] != refs[-1].shape[0]
    prior = refs[0] if has_prior else None
    basis, sums = refs[-2:]
    owned, rank = owners(as_line(picks), devices, local_terms)
    first = lax.broadcasted_iota(jnp.int32, owned.shape, 0).astype(F32) * SLOTS
    slot = jnp.sum(owned * rank, axis=0, keepdims=True)
    slot = slot - (place[1] * SLOTS).astype(F32)
    target = slot + jnp.sum(owned * first, axis=0, keepdims=True)
    target = jnp.where((slot >= 0.0) & (slot < SLOTS), target, -1.0)
    count = target.shape[1]
    lines = lax.broadcasted_iota(jnp.int32, (devices * SLOTS, count), 0).astype(F32)
    moved = (lines == target).astype(F32).astype(BF16)
    columns = lax.dot_general(
        moved, slots[...], (((0,), (0,)), ((), ())), preferred_element_type=F32
    )
    if has_prior:
        columns = columns + prior[...].astype(F32)
    basis[...] = columns.astype(BF16)

    def fill(side):
        row = 0
        for top, bottom, start, stop in HALVES[side]:
            strip = lax.dot_general(
                basis[top:bottom],
                basis[start:stop],
                (((1,), (1,)), ((), ())),
                preferred_element_type=F32,
            )
            for j in range(0, stop - start, BLOCK):
                after = row + bottom - top
                piece = strip[:, j : j + BLOCK]
                sums[row:after, :] = piece if own else piece + other[row:after, :]
                row = after
        if not own:
            sums[row:, :] = other[row:, :]
            return
        resp = other.shape[0]
        inner = split_dot(other[...], basis[...], ((1,), (1,)))
        for j in range(0, count, BLOCK):
            sums[row : row + resp, :] = inner[:, j : j + BLOCK]
            row += resp
        sums[row:, :] = jnp.zeros((sums.shape[0] - row, LANES), F32)

    for side in range(2):
        pl.when(place[2] == side)(functools.partial(fill, side))


def gram(place, picks, slots, other, local_terms, half, prior=None):
    devices, _, rows = slots.shape
    count = picks.size
    extra = () if prior is None else (prior,)
    operands = (place, picks, slots.reshape(-1, rows), other, *extra)
    return call(
        functools.partial(gram_kernel, local_terms, devices, prior is not None),
        "gram",
        (
            jax.ShapeDtypeStruct((count, rows), BF16),
            jax.ShapeDtypeStruct((half, LANES), F32),
        ),
        [SCALAR] + [WHOLE] * (len(operands) - 1),
        (WHOLE, WHOLE),
        cost_estimate=pl.CostEstimate(
            flops=2 * count * rows * (devices * SLOTS + count),
            bytes_accessed=2 * count * rows,
            transcendentals=0,
        ),
    )(*operands)


def split_dot(left, right, dims):
    rows = left.shape[0]
    rest, parts = left, []
    for _ in range(3):
        part = rest.astype(BF16).astype(F32)
        parts.append(part)
        rest = rest - part
    out = lax.dot_general(
        jnp.concatenate(parts, axis=0).astype(BF16),
        right,
        (dims, ((), ())),
        preferred_element_type=F32,
    )
    return out[2 * rows :] + out[rows : 2 * rows] + out[:rows]


def total_kernel(pieces, totals):
    total = jnp.sum(pieces[...], axis=0)
    for piece in range(totals.shape[0]):
        totals[piece] = total


def totals(pieces):
    shape = jax.ShapeDtypeStruct(pieces.shape, pieces.dtype)
    return call(total_kernel, "totals", shape, [WHOLE], WHOLE)(pieces)


def spread(piece):
    return jnp.broadcast_to(piece, (SUB, LANES))


def dot(left, right):
    return jnp.dot(left, right, precision=HIGH, preferred_element_type=F32)


def dot_first(left, right):
    return lax.dot_general(
        left,
        right,
        (((0,), (0,)), ((), ())),
        precision=HIGH,
        preferred_element_type=F32,
    )


def across(group, lane):
    index = jnp.full((SUB, LANES), lane, jnp.int32)
    return jnp.take_along_axis(group, index, axis=1, mode="promise_in_bounds")


def invert_small(columns, sub):
    for i in range(SUB):
        pivot = 1.0 / spread(columns[i][i : i + 1, :])
        column, here = columns[i], sub == i
        after = []
        for j in range(SUB):
            if j == i:
                after.append(jnp.where(here, pivot, -column * pivot))
            else:
                factor = spread(columns[j][i : i + 1, :]) * pivot
                after.append(jnp.where(here, factor, columns[j] - column * factor))
        columns = after
    return columns


def invert_block(groups):
    lane = lax.broadcasted_iota(jnp.int32, (SUB, LANES), 1)
    sub = lax.broadcasted_iota(jnp.int32, (SUB, LANES), 0)
    groups = list(groups)
    count = len(groups)
    for k in range(count):
        first = SUB * k
        mine = groups[k]
        small = invert_small(
            [across(mine, first + j) for j in range(SUB)], sub
        )
        inside = (lane >= first) & (lane < first + SUB)
        unit = jnp.where(lane - first == sub, 1.0, 0.0)
        mine = jnp.where(inside, unit, mine)
        top = small[0] * spread(mine[0:1, :])
        for j in range(1, SUB):
            top = top + small[j] * spread(mine[j : j + 1, :])
        rows = [spread(top[j : j + 1, :]) for j in range(SUB)]
        for step in range(1, count):
            g = (k + step) % count
            new = jnp.where(inside, 0.0, groups[g])
            for j in range(SUB):
                new = new - across(groups[g], first + j) * rows[j]
            groups[g] = new
        groups[k] = top
    return groups


def groups_of(block):
    return [block[SUB * g : SUB * (g + 1), :] for g in range(BLOCK // SUB)]


def first_kernel(sums, inverse):
    for g, group in enumerate(invert_block(groups_of(sums[:BLOCK, :]))):
        inverse[SUB * g : SUB * (g + 1), :] = group


def first_inverse(sums):
    return call(
        first_kernel,
        "first_inverse",
        jax.ShapeDtypeStruct((BLOCK, BLOCK), F32),
        [WHOLE],
        WHOLE,
        cost_estimate=pl.CostEstimate(
            flops=2 * 10**9, bytes_accessed=10**5, transcendentals=0
        ),
    )(sums)


def finish_kernel(scale, place, *refs):
    mine, other, known_inverse, responses, basis, design, residual, pieces = refs[:8]
    work, inverse, coef, held, sem = refs[8:]
    count = basis.shape[0]
    resp = responses.shape[0]
    blocks = count // BLOCK
    core = place[2]
    copy = pltpu.make_async_copy(design, held, sem)
    copy.start()

    def place_side(side, source):
        row = 0
        for top, bottom, start, stop in HALVES[side]:
            for j in range(start, stop, BLOCK):
                after = row + bottom - top
                work[top:bottom, j : j + BLOCK] = source[row:after, :]
                row = after

    for side in range(2):
        pl.when(core == side)(functools.partial(place_side, side, mine))
        pl.when(core != side)(functools.partial(place_side, side, other))
    for i in range(blocks):
        at = pl.ds(INNER + i * resp, resp)
        tall = [mine[at, :] + other[at, :], jnp.zeros((BLOCK - resp, BLOCK), F32)]
        work[i * BLOCK : (i + 1) * BLOCK, count:] = jnp.concatenate(tall, axis=0).T

    def eliminate(k):
        start, stop = k * BLOCK, (k + 1) * BLOCK
        right = work[start:stop, stop:]
        lead = dot(inverse[...], right)
        if stop < count:
            work[stop:, stop:] = work[stop:, stop:] - dot_first(
                right[:, : count - stop], lead
            )
        work[start:stop, stop:] = lead

    def step(k, carry):
        start = pl.multiple_of(k * BLOCK, BLOCK)
        groups = [
            work[pl.ds(pl.multiple_of(start + SUB * g, SUB), SUB), pl.ds(start, BLOCK)]
            for g in range(BLOCK // SUB)
        ]
        for g, group in enumerate(invert_block(groups)):
            inverse[SUB * g : SUB * (g + 1), :] = group
        for known in range(1, blocks):
            pl.when(k == known)(functools.partial(eliminate, known))
        return carry

    inverse[...] = known_inverse[...]
    eliminate(0)
    lax.fori_loop(1, blocks, step, 0)
    coef[count - BLOCK :, :] = work[count - BLOCK :, count:]
    for k in reversed(range(blocks - 1)):
        start, stop = k * BLOCK, (k + 1) * BLOCK
        coef[start:stop, :] = work[start:stop, count:] - dot(
            work[start:stop, stop:count], coef[stop:, :]
        )
    fitted = split_dot(coef[...].T[:resp, :], basis[...], ((1,), (0,)))
    left = responses[...] - fitted
    residual[...] = left
    rounded = left.astype(BF16)
    tiles = design.shape[1] // LANES
    copy.wait()
    for tile in range(0, tiles, 2):
        part = held[:, tile * LANES : (tile + 2) * LANES]
        both = jnp.dot(rounded, part, preferred_element_type=F32) * scale
        pieces[tile] = both[:, :LANES]
        pieces[tile + 1] = both[:, LANES:]
    pieces[tiles:] = jnp.zeros((pieces.shape[0] - tiles, resp, LANES), F32)


def finish(place, mine, other, inverse, responses, basis, design, pieces, scale):
    resp, rows = responses.shape
    count = basis.shape[0]
    return call(
        functools.partial(finish_kernel, scale),
        "finish",
        (
            jax.ShapeDtypeStruct((resp, rows), F32),
            jax.ShapeDtypeStruct((pieces, resp, LANES), F32),
        ),
        [SCALAR] + [WHOLE] * 5 + [pl.BlockSpec(memory_space=pltpu.HBM)],
        (WHOLE, WHOLE),
        [
            pltpu.VMEM((count, count + LANES), F32),
            pltpu.VMEM((BLOCK, BLOCK), F32),
            pltpu.VMEM((count, LANES), F32),
            pltpu.VMEM(design.shape, design.dtype),
            pltpu.SemaphoreType.DMA,
        ],
    )(place, mine, other, inverse, responses, basis, design)


def summed_everywhere(pieces, axis, groups=None):
    return exchange(totals(exchange(pieces, axis, groups)), axis, groups)


def local(design, responses, picks):
    run_devices, term_devices = lax.axis_size("runs"), lax.axis_size("terms")
    resp, local_rows = responses.shape
    local_terms = design.shape[1]
    chips = run_devices // 2
    core = lax.axis_index("runs") % 2
    swap = [(i, i ^ 1) for i in range(run_devices)]
    sides = [list(range(side, run_devices, 2)) for side in range(2)]
    count = picks.size
    half = (4 + 2) * BLOCK

    def fetch(turn):
        where = jnp.stack([lax.axis_index("terms"), jnp.int32(turn), core])
        packed, most = pack(where, picks, design, term_devices)
        return where, exchange(packed, "terms"), most

    def grams(where, slots, prior=(None, None)):
        partner_slots = lax.ppermute(slots, "runs", swap)
        basis, sums = gram(
            where, picks, slots, responses, local_terms, half, prior[0]
        )
        partner_basis, sums = gram(
            where, picks, partner_slots, sums, local_terms, half, prior[1]
        )
        return basis, partner_basis, sums

    at, slots, most = fetch(0)
    state = grams(at, slots)

    def another(carry):
        turn, basis, partner_basis, _ = carry
        where, more, _ = fetch(turn)
        return turn + 1, *grams(where, more, (basis, partner_basis))

    _, basis, _, sums = lax.while_loop(
        lambda carry: carry[0] * SLOTS < most[0], another, (jnp.int32(1), *state)
    )

    mine = summed_everywhere(sums.reshape(chips, -1, LANES), "runs", sides)
    mine = mine.reshape(half, LANES)
    other = lax.ppermute(mine, "runs", swap)
    inverse = first_inverse(mine)

    scale = float(local_rows * run_devices) ** -0.5
    residual, pieces = finish(
        at, mine, other, inverse, responses, basis, design, run_devices, scale
    )
    gathered = summed_everywhere(pieces, "runs")[: local_terms // LANES]
    correlations = gathered.transpose(1, 0, 2).reshape(resp, -1)
    return (residual, correlations)


def solution(mesh):
    placed = (P("runs", "terms"), P(None, "runs"), P())
    return jax.shard_map(
        local,
        mesh=mesh,
        in_specs=placed,
        out_specs=(P(None, "runs"), P(None, "terms")),
        check_vma=False,
    )
```

```python
import functools

import jax
import jax.numpy as jnp
from jax import lax
from jax.experimental import pallas as pl
from jax.experimental.pallas import tpu as pltpu
from jax.sharding import PartitionSpec as P

LANES = 128
SUB = 8
BLOCK = 128
SLOTS = 96
CHUNKS = 2
HALVES = (
    ((0, 128, 0, 512), (128, 256, 128, 256), (128, 192, 256, 384)),
    (
        (0, 128, 0, 128),
        (192, 256, 256, 384),
        (128, 256, 384, 512),
        (256, 384, 256, 512),
        (384, 512, 384, 512),
    ),
)
INNER = 704
F32 = jnp.float32
BF16 = jnp.bfloat16


def call(kernel, name, out_shape, in_specs, out_specs, scratch=(), vmem=32, **more):
    return pl.pallas_call(
        kernel,
        out_shape=out_shape,
        in_specs=in_specs,
        out_specs=out_specs,
        scratch_shapes=scratch,
        compiler_params=pltpu.CompilerParams(vmem_limit_bytes=vmem * 2**20),
        name=name,
        **more,
    )


WHOLE = pl.BlockSpec(memory_space=pltpu.VMEM)
SCALAR = pl.BlockSpec(memory_space=pltpu.SMEM)


def exchange(pieces, axis, groups=None):
    return lax.all_to_all(pieces, axis, 0, 0, axis_index_groups=groups)


def as_line(picks):
    return jnp.concatenate([picks[i : i + 1, :] for i in range(picks.shape[0])], axis=1)


def owners(picks, devices, local_terms):
    count = picks.shape[1]
    first = lax.broadcasted_iota(jnp.int32, (devices, count), 0) * local_terms
    owned = ((picks >= first) & (picks < first + local_terms)).astype(F32)
    before = lax.broadcasted_iota(jnp.int32, (count, count), 0)
    after = lax.broadcasted_iota(jnp.int32, (count, count), 1)
    rank = jnp.dot(
        owned.astype(BF16),
        (before < after).astype(F32).astype(BF16),
        preferred_element_type=F32,
    )
    return owned, rank


def pack_kernel(place, picks, design, packed, most, held, where, sems):
    devices = packed.shape[0]
    local_terms = design.shape[1]
    chunk = local_terms // CHUNKS

    def part(step):
        columns = pl.ds(step * chunk, chunk)
        return pltpu.make_async_copy(
            design.at[:, columns], held.at[:, columns], sems.at[step]
        )

    for step in range(CHUNKS):
        part(step).start()
    line = as_line(picks)
    owned, rank = owners(line, devices, local_terms)
    counts = jnp.sum(owned, axis=1, keepdims=True)
    most[0] = jnp.max(counts).astype(jnp.int32)
    me = lax.broadcasted_iota(jnp.int32, owned.shape, 0) == place[0]
    mine = jnp.where(me, owned, 0.0)
    slot = jnp.sum(mine * rank, axis=0, keepdims=True)
    slot = slot - (place[1] * SLOTS).astype(F32)
    slot = jnp.where(jnp.sum(mine, axis=0, keepdims=True) > 0.0, slot, -1.0)
    slots = lax.broadcasted_iota(jnp.int32, (SLOTS, slot.shape[1]), 0).astype(F32)
    inner = (line - place[0] * local_terms + 1).astype(F32)
    inner = jnp.where(slots == slot, inner, 0.0)
    where[...] = jnp.sum(inner, axis=1, keepdims=True).astype(jnp.int32) - 1
    total = jnp.zeros((SLOTS, design.shape[0]), F32)
    for step in range(CHUNKS):
        columns = lax.broadcasted_iota(jnp.int32, (SLOTS, chunk), 1) + step * chunk
        chosen = (columns == where[...]).astype(F32).astype(BF16)
        part(step).wait()
        total = total + lax.dot_general(
            chosen,
            held[:, step * chunk : (step + 1) * chunk],
            (((1,), (1,)), ((), ())),
            preferred_element_type=F32,
        )
    value = total.astype(BF16)
    for partner in range(devices):
        packed[partner] = value


def pack(place, picks, design, devices):
    rows = design.shape[0]
    return call(
        pack_kernel,
        "pack",
        (
            jax.ShapeDtypeStruct((devices, SLOTS, rows), BF16),
            jax.ShapeDtypeStruct((1,), jnp.int32),
        ),
        [SCALAR, WHOLE, pl.BlockSpec(memory_space=pltpu.HBM)],
        (WHOLE, SCALAR),
        [
            pltpu.VMEM(design.shape, design.dtype),
            pltpu.VMEM((SLOTS, 1), jnp.int32),
            pltpu.SemaphoreType.DMA((CHUNKS,)),
        ],
    )(place, picks, design)


def gram_kernel(local_terms, devices, has_prior, place, picks, slots, other, *refs):
    own = other.shape[0] != refs[-1].shape[0]
    prior = refs[0] if has_prior else None
    basis, sums = refs[-2:]
    owned, rank = owners(as_line(picks), devices, local_terms)
    first = lax.broadcasted_iota(jnp.int32, owned.shape, 0).astype(F32) * SLOTS
    slot = jnp.sum(owned * rank, axis=0, keepdims=True)
    slot = slot - (place[1] * SLOTS).astype(F32)
    target = slot + jnp.sum(owned * first, axis=0, keepdims=True)
    target = jnp.where((slot >= 0.0) & (slot < SLOTS), target, -1.0)
    count = target.shape[1]
    lines = lax.broadcasted_iota(jnp.int32, (devices * SLOTS, count), 0).astype(F32)
    moved = (lines == target).astype(F32).astype(BF16)
    columns = lax.dot_general(
        moved, slots[...], (((0,), (0,)), ((), ())), preferred_element_type=F32
    )
    if has_prior:
        columns = columns + prior[...].astype(F32)
    basis[...] = columns.astype(BF16)

    def fill(side):
        row = 0
        for top, bottom, start, stop in HALVES[side]:
            strip = lax.dot_general(
                basis[top:bottom],
                basis[start:stop],
                (((1,), (1,)), ((), ())),
                preferred_element_type=F32,
            )
            for j in range(0, stop - start, BLOCK):
                after = row + bottom - top
                piece = strip[:, j : j + BLOCK]
                sums[row:after, :] = piece if own else piece + other[row:after, :]
                row = after
        if not own:
            sums[row:, :] = other[row:, :]
            return
        resp = other.shape[0]
        inner = split_dot(other[...], basis[...], ((1,), (1,)))
        for j in range(0, count, BLOCK):
            sums[row : row + resp, :] = inner[:, j : j + BLOCK]
            row += resp
        sums[row:, :] = jnp.zeros((sums.shape[0] - row, LANES), F32)

    for side in range(2):
        pl.when(place[2] == side)(functools.partial(fill, side))


def gram(place, picks, slots, other, local_terms, half, prior=None):
    devices, _, rows = slots.shape
    count = picks.size
    extra = () if prior is None else (prior,)
    operands = (place, picks, slots.reshape(-1, rows), other, *extra)
    return call(
        functools.partial(gram_kernel, local_terms, devices, prior is not None),
        "gram",
        (
            jax.ShapeDtypeStruct((count, rows), BF16),
            jax.ShapeDtypeStruct((half, LANES), F32),
        ),
        [SCALAR] + [WHOLE] * (len(operands) - 1),
        (WHOLE, WHOLE),
        cost_estimate=pl.CostEstimate(
            flops=2 * count * rows * (devices * SLOTS + count),
            bytes_accessed=2 * count * rows,
            transcendentals=0,
        ),
    )(*operands)


def split(value):
    parts = []
    for _ in range(3):
        parts.append(value.astype(BF16).astype(F32))
        value = value - parts[-1]
    return parts


def left_parts(value, axis):
    a, b, c = split(value)
    return jnp.concatenate([a, a, a, b, b, c], axis=axis).astype(BF16)


def right_parts(value):
    a, b, c = split(value)
    return jnp.concatenate([a, b, c, a, b, a], axis=0).astype(BF16)


def dot_parts(left, right, axis=1):
    return lax.dot_general(
        left, right, (((axis,), (0,)), ((), ())), preferred_element_type=F32
    )


def dot(left, right):
    return dot_parts(left_parts(left, 1), right_parts(right))


def split_dot(left, right, dims):
    rows = left.shape[0]
    out = lax.dot_general(
        jnp.concatenate(split(left), axis=0).astype(BF16),
        right,
        (dims, ((), ())),
        preferred_element_type=F32,
    )
    return out[2 * rows :] + out[rows : 2 * rows] + out[:rows]


def total_kernel(pieces, totals):
    total = jnp.sum(pieces[...], axis=0)
    for piece in range(totals.shape[0]):
        totals[piece] = total


def totals(pieces):
    shape = jax.ShapeDtypeStruct(pieces.shape, pieces.dtype)
    return call(total_kernel, "totals", shape, [WHOLE], WHOLE)(pieces)


def spread(piece):
    return jnp.broadcast_to(piece, (SUB, LANES))


def across(group, lane):
    index = jnp.full((SUB, LANES), lane, jnp.int32)
    return jnp.take_along_axis(group, index, axis=1, mode="promise_in_bounds")


def invert_small(columns, sub):
    for i in range(SUB):
        pivot = 1.0 / spread(columns[i][i : i + 1, :])
        column, here = columns[i], sub == i
        after = []
        for j in range(SUB):
            if j == i:
                after.append(jnp.where(here, pivot, -column * pivot))
            else:
                factor = spread(columns[j][i : i + 1, :]) * pivot
                after.append(jnp.where(here, factor, columns[j] - column * factor))
        columns = after
    return columns


def invert_block(groups):
    lane = lax.broadcasted_iota(jnp.int32, (SUB, LANES), 1)
    sub = lax.broadcasted_iota(jnp.int32, (SUB, LANES), 0)
    groups = list(groups)
    count = len(groups)
    for k in range(count):
        first = SUB * k
        mine = groups[k]
        turned = left_parts(jnp.where(lane < first, -mine, mine), 0)
        small = invert_small([across(mine, first + j) for j in range(SUB)], sub)
        inside = (lane >= first) & (lane < first + SUB)
        unit = jnp.where(lane - first == sub, 1.0, 0.0)
        mine = jnp.where(inside, unit, mine)
        terms = [small[j] * spread(mine[j : j + 1, :]) for j in range(SUB)]
        while len(terms) > 1:
            terms = [terms[i] + terms[i + 1] for i in range(0, len(terms), 2)]
        top = terms[0]
        change = dot_parts(turned, right_parts(top), 0)
        for g in range(count):
            new = jnp.where(inside, 0.0, groups[g])
            if g == k + 1:
                for j in range(SUB):
                    row = spread(top[j : j + 1, :])
                    new = new - across(groups[g], first + j) * row
            else:
                new = new - change[SUB * g : SUB * (g + 1), :]
            groups[g] = new
        groups[k] = top
    return groups


def groups_of(block):
    return [block[SUB * g : SUB * (g + 1), :] for g in range(BLOCK // SUB)]


def first_kernel(sums, inverse):
    for g, group in enumerate(invert_block(groups_of(sums[:BLOCK, :]))):
        inverse[SUB * g : SUB * (g + 1), :] = group


def first_inverse(sums):
    return call(
        first_kernel,
        "first_inverse",
        jax.ShapeDtypeStruct((BLOCK, BLOCK), F32),
        [WHOLE],
        WHOLE,
        cost_estimate=pl.CostEstimate(
            flops=2 * 10**9, bytes_accessed=10**5, transcendentals=0
        ),
    )(sums)


def finish_kernel(scale, place, *refs):
    mine, other, known_inverse, responses, basis, design, residual, pieces = refs[:8]
    work, inverse, coef = refs[8:]
    count = basis.shape[0]
    resp = responses.shape[0]
    blocks = count // BLOCK
    core = place[2]

    def place_side(side, source):
        row = 0
        for top, bottom, start, stop in HALVES[side]:
            for j in range(start, stop, BLOCK):
                after = row + bottom - top
                work[top:bottom, j : j + BLOCK] = source[row:after, :]
                row = after

    for side in range(2):
        pl.when(core == side)(functools.partial(place_side, side, mine))
        pl.when(core != side)(functools.partial(place_side, side, other))
    for i in range(blocks):
        at = pl.ds(INNER + i * resp, resp)
        tall = [mine[at, :] + other[at, :], jnp.zeros((BLOCK - resp, BLOCK), F32)]
        work[i * BLOCK : (i + 1) * BLOCK, count:] = jnp.concatenate(tall, axis=0).T

    def eliminate(k):
        start, stop = k * BLOCK, (k + 1) * BLOCK
        right = work[start:stop, stop:]
        lead = dot(inverse[...], right)
        if stop < count:
            turned = right[:, : count - stop].T
            work[stop:, stop:] = work[stop:, stop:] - dot(turned, lead)
        work[start:stop, stop:] = lead

    def step(k, carry):
        start = pl.multiple_of(k * BLOCK, BLOCK)
        groups = [
            work[pl.ds(pl.multiple_of(start + SUB * g, SUB), SUB), pl.ds(start, BLOCK)]
            for g in range(BLOCK // SUB)
        ]
        for g, group in enumerate(invert_block(groups)):
            inverse[SUB * g : SUB * (g + 1), :] = group
        for known in range(1, blocks):
            pl.when(k == known)(functools.partial(eliminate, known))
        return carry

    inverse[...] = known_inverse[...]
    eliminate(0)
    lax.fori_loop(1, blocks, step, 0)
    coef[count - BLOCK :, :] = work[count - BLOCK :, count:]
    for k in reversed(range(blocks - 1)):
        start, stop = k * BLOCK, (k + 1) * BLOCK
        coef[start:stop, :] = work[start:stop, count:] - dot(
            work[start:stop, stop:count], coef[stop:, :]
        )
    fitted = split_dot(coef[...].T[:resp, :], basis[...], ((1,), (0,)))
    left = responses[...] - fitted
    residual[...] = left
    rounded = left.astype(BF16)
    tiles = design.shape[1] // LANES
    for tile in range(0, tiles, 2):
        part = design[:, tile * LANES : (tile + 2) * LANES]
        both = jnp.dot(rounded, part, preferred_element_type=F32) * scale
        pieces[tile] = both[:, :LANES]
        pieces[tile + 1] = both[:, LANES:]
    pieces[tiles:] = jnp.zeros((pieces.shape[0] - tiles, resp, LANES), F32)


def finish(place, mine, other, inverse, responses, basis, design, pieces, scale):
    resp, rows = responses.shape
    count = basis.shape[0]
    return call(
        functools.partial(finish_kernel, scale),
        "finish",
        (
            jax.ShapeDtypeStruct((resp, rows), F32),
            jax.ShapeDtypeStruct((pieces, resp, LANES), F32),
        ),
        [SCALAR] + [WHOLE] * 6,
        (WHOLE, WHOLE),
        [
            pltpu.VMEM((count, count + LANES), F32),
            pltpu.VMEM((BLOCK, BLOCK), F32),
            pltpu.VMEM((count, LANES), F32),
        ],
    )(place, mine, other, inverse, responses, basis, design)


def summed_everywhere(pieces, axis, groups=None):
    return exchange(totals(exchange(pieces, axis, groups)), axis, groups)


def local(design, responses, picks):
    run_devices, term_devices = lax.axis_size("runs"), lax.axis_size("terms")
    resp, local_rows = responses.shape
    local_terms = design.shape[1]
    chips = run_devices // 2
    core = lax.axis_index("runs") % 2
    swap = [(i, i ^ 1) for i in range(run_devices)]
    sides = [list(range(side, run_devices, 2)) for side in range(2)]
    count = picks.size
    half = (4 + 2) * BLOCK

    def fetch(turn):
        where = jnp.stack([lax.axis_index("terms"), jnp.int32(turn), core])
        packed, most = pack(where, picks, design, term_devices)
        return where, exchange(packed, "terms"), most

    def grams(where, slots, prior=(None, None)):
        partner_slots = lax.ppermute(slots, "runs", swap)
        basis, sums = gram(
            where, picks, slots, responses, local_terms, half, prior[0]
        )
        partner_basis, sums = gram(
            where, picks, partner_slots, sums, local_terms, half, prior[1]
        )
        return basis, partner_basis, sums

    at, slots, most = fetch(0)
    state = grams(at, slots)

    def another(carry):
        turn, basis, partner_basis, _ = carry
        where, more, _ = fetch(turn)
        return turn + 1, *grams(where, more, (basis, partner_basis))

    _, basis, _, sums = lax.while_loop(
        lambda carry: carry[0] * SLOTS < most[0], another, (jnp.int32(1), *state)
    )

    mine = summed_everywhere(sums.reshape(chips, -1, LANES), "runs", sides)
    mine = mine.reshape(half, LANES)
    other = lax.ppermute(mine, "runs", swap)
    inverse = first_inverse(mine)

    scale = float(local_rows * run_devices) ** -0.5
    residual, pieces = finish(
        at, mine, other, inverse, responses, basis, design, run_devices, scale
    )
    gathered = summed_everywhere(pieces, "runs")[: local_terms // LANES]
    correlations = gathered.transpose(1, 0, 2).reshape(resp, -1)
    return (residual, correlations)


def solution(mesh):
    placed = (P("runs", "terms"), P(None, "runs"), P())
    return jax.shard_map(
        local,
        mesh=mesh,
        in_specs=placed,
        out_specs=(P(None, "runs"), P(None, "terms")),
        check_vma=False,
    )
```

```python
import functools

import jax
import jax.numpy as jnp
from jax import lax
from jax.experimental import pallas as pl
from jax.experimental.pallas import tpu as pltpu
from jax.sharding import PartitionSpec as P

LANES = 128
SUB = 8
BLOCK = 128
SLOTS = 96
CHUNKS = 2
HALVES = (
    ((0, 128, 0, 512), (128, 256, 128, 256), (128, 192, 256, 384)),
    (
        (0, 128, 0, 128),
        (192, 256, 256, 384),
        (128, 256, 384, 512),
        (256, 384, 256, 512),
        (384, 512, 384, 512),
    ),
)
INNER = 704
F32 = jnp.float32
BF16 = jnp.bfloat16


def call(kernel, name, out_shape, in_specs, out_specs, scratch=(), vmem=32, **more):
    return pl.pallas_call(
        kernel,
        out_shape=out_shape,
        in_specs=in_specs,
        out_specs=out_specs,
        scratch_shapes=scratch,
        compiler_params=pltpu.CompilerParams(vmem_limit_bytes=vmem * 2**20),
        name=name,
        **more,
    )


WHOLE = pl.BlockSpec(memory_space=pltpu.VMEM)
SCALAR = pl.BlockSpec(memory_space=pltpu.SMEM)


def exchange(pieces, axis, groups=None):
    return lax.all_to_all(pieces, axis, 0, 0, axis_index_groups=groups)


def as_line(picks):
    return jnp.concatenate([picks[i : i + 1, :] for i in range(picks.shape[0])], axis=1)


def owners(picks, devices, local_terms):
    count = picks.shape[1]
    first = lax.broadcasted_iota(jnp.int32, (devices, count), 0) * local_terms
    owned = ((picks >= first) & (picks < first + local_terms)).astype(F32)
    before = lax.broadcasted_iota(jnp.int32, (count, count), 0)
    after = lax.broadcasted_iota(jnp.int32, (count, count), 1)
    rank = jnp.dot(
        owned.astype(BF16),
        (before < after).astype(F32).astype(BF16),
        preferred_element_type=F32,
    )
    return owned, rank


def pack_kernel(place, picks, design, packed, most, held, where, sems):
    devices = packed.shape[0]
    local_terms = design.shape[1]
    chunk = local_terms // CHUNKS

    def part(step):
        columns = pl.ds(step * chunk, chunk)
        return pltpu.make_async_copy(
            design.at[:, columns], held.at[:, columns], sems.at[step]
        )

    for step in range(CHUNKS):
        part(step).start()
    line = as_line(picks)
    owned, rank = owners(line, devices, local_terms)
    counts = jnp.sum(owned, axis=1, keepdims=True)
    most[0] = jnp.max(counts).astype(jnp.int32)
    me = lax.broadcasted_iota(jnp.int32, owned.shape, 0) == place[0]
    mine = jnp.where(me, owned, 0.0)
    slot = jnp.sum(mine * rank, axis=0, keepdims=True)
    slot = slot - (place[1] * SLOTS).astype(F32)
    slot = jnp.where(jnp.sum(mine, axis=0, keepdims=True) > 0.0, slot, -1.0)
    slots = lax.broadcasted_iota(jnp.int32, (SLOTS, slot.shape[1]), 0).astype(F32)
    inner = (line - place[0] * local_terms + 1).astype(F32)
    inner = jnp.where(slots == slot, inner, 0.0)
    where[...] = jnp.sum(inner, axis=1, keepdims=True).astype(jnp.int32) - 1
    total = jnp.zeros((SLOTS, design.shape[0]), F32)
    for step in range(CHUNKS):
        columns = lax.broadcasted_iota(jnp.int32, (SLOTS, chunk), 1) + step * chunk
        chosen = (columns == where[...]).astype(F32).astype(BF16)
        part(step).wait()
        total = total + lax.dot_general(
            chosen,
            held[:, step * chunk : (step + 1) * chunk],
            (((1,), (1,)), ((), ())),
            preferred_element_type=F32,
        )
    value = total.astype(BF16)
    for partner in range(devices):
        packed[partner] = value


def pack(place, picks, design, devices):
    rows = design.shape[0]
    return call(
        pack_kernel,
        "pack",
        (
            jax.ShapeDtypeStruct((devices, SLOTS, rows), BF16),
            jax.ShapeDtypeStruct((1,), jnp.int32),
        ),
        [SCALAR, WHOLE, pl.BlockSpec(memory_space=pltpu.HBM)],
        (WHOLE, SCALAR),
        [
            pltpu.VMEM(design.shape, design.dtype),
            pltpu.VMEM((SLOTS, 1), jnp.int32),
            pltpu.SemaphoreType.DMA((CHUNKS,)),
        ],
    )(place, picks, design)


def gram_kernel(local_terms, devices, has_prior, place, picks, slots, other, *refs):
    own = other.shape[0] != refs[-1].shape[0]
    prior = refs[0] if has_prior else None
    basis, sums = refs[-2:]
    owned, rank = owners(as_line(picks), devices, local_terms)
    first = lax.broadcasted_iota(jnp.int32, owned.shape, 0).astype(F32) * SLOTS
    slot = jnp.sum(owned * rank, axis=0, keepdims=True)
    slot = slot - (place[1] * SLOTS).astype(F32)
    target = slot + jnp.sum(owned * first, axis=0, keepdims=True)
    target = jnp.where((slot >= 0.0) & (slot < SLOTS), target, -1.0)
    count = target.shape[1]
    lines = lax.broadcasted_iota(jnp.int32, (devices * SLOTS, count), 0).astype(F32)
    moved = (lines == target).astype(F32).astype(BF16)
    columns = lax.dot_general(
        moved, slots[...], (((0,), (0,)), ((), ())), preferred_element_type=F32
    )
    if has_prior:
        columns = columns + prior[...].astype(F32)
    basis[...] = columns.astype(BF16)

    def fill(side):
        row = 0
        for top, bottom, start, stop in HALVES[side]:
            strip = lax.dot_general(
                basis[top:bottom],
                basis[start:stop],
                (((1,), (1,)), ((), ())),
                preferred_element_type=F32,
            )
            for j in range(0, stop - start, BLOCK):
                after = row + bottom - top
                piece = strip[:, j : j + BLOCK]
                sums[row:after, :] = piece if own else piece + other[row:after, :]
                row = after
        if not own:
            sums[row:, :] = other[row:, :]
            return
        resp = other.shape[0]
        inner = split_dot(other[...], basis[...], ((1,), (1,)))
        for j in range(0, count, BLOCK):
            sums[row : row + resp, :] = inner[:, j : j + BLOCK]
            row += resp
        sums[row:, :] = jnp.zeros((sums.shape[0] - row, LANES), F32)

    for side in range(2):
        pl.when(place[2] == side)(functools.partial(fill, side))


def gram(place, picks, slots, other, local_terms, half, prior=None):
    devices, _, rows = slots.shape
    count = picks.size
    extra = () if prior is None else (prior,)
    operands = (place, picks, slots.reshape(-1, rows), other, *extra)
    return call(
        functools.partial(gram_kernel, local_terms, devices, prior is not None),
        "gram",
        (
            jax.ShapeDtypeStruct((count, rows), BF16),
            jax.ShapeDtypeStruct((half, LANES), F32),
        ),
        [SCALAR] + [WHOLE] * (len(operands) - 1),
        (WHOLE, WHOLE),
        cost_estimate=pl.CostEstimate(
            flops=2 * count * rows * (devices * SLOTS + count),
            bytes_accessed=2 * count * rows,
            transcendentals=0,
        ),
    )(*operands)


def split(value):
    parts = []
    for _ in range(3):
        parts.append(value.astype(BF16).astype(F32))
        value = value - parts[-1]
    return parts


def left_parts(value, axis):
    a, b, c = split(value)
    return jnp.concatenate([a, a, a, b, b, c], axis=axis).astype(BF16)


def right_parts(value):
    a, b, c = split(value)
    return jnp.concatenate([a, b, c, a, b, a], axis=0).astype(BF16)


def dot_parts(left, right, axis=1):
    return lax.dot_general(
        left, right, (((axis,), (0,)), ((), ())), preferred_element_type=F32
    )


def dot(left, right):
    return dot_parts(left_parts(left, 1), right_parts(right))


def split_dot(left, right, dims):
    rows = left.shape[0]
    out = lax.dot_general(
        jnp.concatenate(split(left), axis=0).astype(BF16),
        right,
        (dims, ((), ())),
        preferred_element_type=F32,
    )
    return out[2 * rows :] + out[rows : 2 * rows] + out[:rows]


def total_kernel(pieces, totals):
    total = jnp.sum(pieces[...], axis=0).astype(totals.dtype)
    totals[...] = jnp.broadcast_to(total, totals.shape)


def totals(pieces, sent):
    shape = jax.ShapeDtypeStruct(pieces.shape, sent)
    return call(total_kernel, "totals", shape, [WHOLE], WHOLE)(pieces)


def spread(piece):
    return jnp.broadcast_to(piece, (SUB, LANES))


def across(group, lane):
    index = jnp.full((SUB, LANES), lane, jnp.int32)
    return jnp.take_along_axis(group, index, axis=1, mode="promise_in_bounds")


def invert_small(columns, sub):
    for i in range(SUB):
        pivot = 1.0 / spread(columns[i][i : i + 1, :])
        column, here = columns[i], sub == i
        after = []
        for j in range(SUB):
            if j == i:
                after.append(jnp.where(here, pivot, -column * pivot))
            else:
                factor = spread(columns[j][i : i + 1, :]) * pivot
                after.append(jnp.where(here, factor, columns[j] - column * factor))
        columns = after
    return columns


def invert_block(groups):
    lane = lax.broadcasted_iota(jnp.int32, (SUB, LANES), 1)
    sub = lax.broadcasted_iota(jnp.int32, (SUB, LANES), 0)
    groups = list(groups)
    count = len(groups)
    for k in range(count):
        first = SUB * k
        mine = groups[k]
        turned = left_parts(jnp.where(lane < first, -mine, mine), 0)
        small = invert_small([across(mine, first + j) for j in range(SUB)], sub)
        inside = (lane >= first) & (lane < first + SUB)
        unit = jnp.where(lane - first == sub, 1.0, 0.0)
        mine = jnp.where(inside, unit, mine)
        terms = [small[j] * spread(mine[j : j + 1, :]) for j in range(SUB)]
        while len(terms) > 1:
            terms = [terms[i] + terms[i + 1] for i in range(0, len(terms), 2)]
        top = terms[0]
        change = dot_parts(turned, right_parts(top), 0)
        for g in range(count):
            new = jnp.where(inside, 0.0, groups[g])
            if g == k + 1:
                for j in range(SUB):
                    row = spread(top[j : j + 1, :])
                    new = new - across(groups[g], first + j) * row
            else:
                new = new - change[SUB * g : SUB * (g + 1), :]
            groups[g] = new
        groups[k] = top
    return groups


def groups_of(block):
    return [block[SUB * g : SUB * (g + 1), :] for g in range(BLOCK // SUB)]


def first_kernel(sums, inverse):
    for g, group in enumerate(invert_block(groups_of(sums[:BLOCK, :]))):
        inverse[SUB * g : SUB * (g + 1), :] = group


def first_inverse(sums):
    return call(
        first_kernel,
        "first_inverse",
        jax.ShapeDtypeStruct((BLOCK, BLOCK), F32),
        [WHOLE],
        WHOLE,
        cost_estimate=pl.CostEstimate(
            flops=2 * 10**9, bytes_accessed=10**5, transcendentals=0
        ),
    )(sums)


def finish_kernel(scale, place, *refs):
    mine, other, known_inverse, responses, basis, design, residual, pieces = refs[:8]
    work, inverse, coef = refs[8:]
    count = basis.shape[0]
    resp = responses.shape[0]
    blocks = count // BLOCK
    core = place[2]

    def place_side(side, source):
        row = 0
        for top, bottom, start, stop in HALVES[side]:
            for j in range(start, stop, BLOCK):
                after = row + bottom - top
                work[top:bottom, j : j + BLOCK] = source[row:after, :]
                row = after

    for side in range(2):
        pl.when(core == side)(functools.partial(place_side, side, mine))
        pl.when(core != side)(functools.partial(place_side, side, other))
    for i in range(blocks):
        at = pl.ds(INNER + i * resp, resp)
        tall = [mine[at, :] + other[at, :], jnp.zeros((BLOCK - resp, BLOCK), F32)]
        work[i * BLOCK : (i + 1) * BLOCK, count:] = jnp.concatenate(tall, axis=0).T

    def eliminate(k):
        start, stop = k * BLOCK, (k + 1) * BLOCK
        right = work[start:stop, stop:]
        lead = dot(inverse[...], right)
        if stop < count:
            turned = right[:, : count - stop].T
            work[stop:, stop:] = work[stop:, stop:] - dot(turned, lead)
        work[start:stop, stop:] = lead

    def step(k, carry):
        start = pl.multiple_of(k * BLOCK, BLOCK)
        groups = [
            work[pl.ds(pl.multiple_of(start + SUB * g, SUB), SUB), pl.ds(start, BLOCK)]
            for g in range(BLOCK // SUB)
        ]
        for g, group in enumerate(invert_block(groups)):
            inverse[SUB * g : SUB * (g + 1), :] = group
        for known in range(1, blocks):
            pl.when(k == known)(functools.partial(eliminate, known))
        return carry

    inverse[...] = known_inverse[...]
    eliminate(0)
    lax.fori_loop(1, blocks, step, 0)
    coef[count - BLOCK :, :] = work[count - BLOCK :, count:]
    for k in reversed(range(blocks - 1)):
        start, stop = k * BLOCK, (k + 1) * BLOCK
        coef[start:stop, :] = work[start:stop, count:] - dot(
            work[start:stop, stop:count], coef[stop:, :]
        )
    fitted = split_dot(coef[...].T[:resp, :], basis[...], ((1,), (0,)))
    left = responses[...] - fitted
    residual[...] = left
    rounded = left.astype(BF16)
    tiles = design.shape[1] // LANES
    for tile in range(0, tiles, 2):
        part = design[:, tile * LANES : (tile + 2) * LANES]
        both = jnp.dot(rounded, part, preferred_element_type=F32) * scale
        pieces[tile] = both[:, :LANES]
        pieces[tile + 1] = both[:, LANES:]
    pieces[tiles:] = jnp.zeros((pieces.shape[0] - tiles, resp, LANES), F32)


def finish(place, mine, other, inverse, responses, basis, design, pieces, scale):
    resp, rows = responses.shape
    count = basis.shape[0]
    return call(
        functools.partial(finish_kernel, scale),
        "finish",
        (
            jax.ShapeDtypeStruct((resp, rows), F32),
            jax.ShapeDtypeStruct((pieces, resp, LANES), F32),
        ),
        [SCALAR] + [WHOLE] * 6,
        (WHOLE, WHOLE),
        [
            pltpu.VMEM((count, count + LANES), F32),
            pltpu.VMEM((BLOCK, BLOCK), F32),
            pltpu.VMEM((count, LANES), F32),
        ],
    )(place, mine, other, inverse, responses, basis, design)


def summed_everywhere(pieces, axis, groups=None, sent=F32):
    return exchange(totals(exchange(pieces, axis, groups), sent), axis, groups)


def local(design, responses, picks):
    run_devices, term_devices = lax.axis_size("runs"), lax.axis_size("terms")
    resp, local_rows = responses.shape
    local_terms = design.shape[1]
    chips = run_devices // 2
    core = lax.axis_index("runs") % 2
    swap = [(i, i ^ 1) for i in range(run_devices)]
    sides = [list(range(side, run_devices, 2)) for side in range(2)]
    count = picks.size
    half = (4 + 2) * BLOCK

    def fetch(turn):
        where = jnp.stack([lax.axis_index("terms"), jnp.int32(turn), core])
        packed, most = pack(where, picks, design, term_devices)
        return where, exchange(packed, "terms"), most

    def grams(where, slots, prior=(None, None)):
        partner_slots = lax.ppermute(slots, "runs", swap)
        basis, sums = gram(
            where, picks, slots, responses, local_terms, half, prior[0]
        )
        partner_basis, sums = gram(
            where, picks, partner_slots, sums, local_terms, half, prior[1]
        )
        return basis, partner_basis, sums

    at, slots, most = fetch(0)
    state = grams(at, slots)

    def another(carry):
        turn, basis, partner_basis, _ = carry
        where, more, _ = fetch(turn)
        return turn + 1, *grams(where, more, (basis, partner_basis))

    _, basis, _, sums = lax.while_loop(
        lambda carry: carry[0] * SLOTS < most[0], another, (jnp.int32(1), *state)
    )

    mine = summed_everywhere(sums.reshape(chips, -1, LANES), "runs", sides)
    mine = mine.reshape(half, LANES)
    other = lax.ppermute(mine, "runs", swap)
    inverse = first_inverse(mine)

    scale = float(local_rows * run_devices) ** -0.5
    residual, pieces = finish(
        at, mine, other, inverse, responses, basis, design, run_devices, scale
    )
    gathered = summed_everywhere(pieces, "runs", sent=BF16)[: local_terms // LANES]
    correlations = gathered.transpose(1, 0, 2).reshape(resp, -1).astype(F32)
    return (residual, correlations)


def solution(mesh):
    placed = (P("runs", "terms"), P(None, "runs"), P())
    return jax.shard_map(
        local,
        mesh=mesh,
        in_specs=placed,
        out_specs=(P(None, "runs"), P(None, "terms")),
        check_vma=False,
    )
```

```python
import functools

import jax
import jax.numpy as jnp
from jax import lax
from jax.experimental import pallas as pl
from jax.experimental.pallas import tpu as pltpu
from jax.sharding import PartitionSpec as P

LANES = 128
SUB = 8
BLOCK = 128
SLOTS = 96
CHUNKS = 2
HALVES = (
    ((0, 128, 0, 512), (128, 256, 128, 256), (128, 192, 256, 384)),
    (
        (0, 128, 0, 128),
        (192, 256, 256, 384),
        (128, 256, 384, 512),
        (256, 384, 256, 512),
        (384, 512, 384, 512),
    ),
)
INNER = 704
F32 = jnp.float32
BF16 = jnp.bfloat16


def call(kernel, name, out_shape, in_specs, out_specs, scratch=(), vmem=32, **more):
    return pl.pallas_call(
        kernel,
        out_shape=out_shape,
        in_specs=in_specs,
        out_specs=out_specs,
        scratch_shapes=scratch,
        compiler_params=pltpu.CompilerParams(vmem_limit_bytes=vmem * 2**20),
        name=name,
        **more,
    )


WHOLE = pl.BlockSpec(memory_space=pltpu.VMEM)
SCALAR = pl.BlockSpec(memory_space=pltpu.SMEM)


def exchange(pieces, axis, groups=None):
    return lax.all_to_all(pieces, axis, 0, 0, axis_index_groups=groups)


def as_line(picks):
    return jnp.concatenate([picks[i : i + 1, :] for i in range(picks.shape[0])], axis=1)


def owners(picks, devices, local_terms):
    count = picks.shape[1]
    first = lax.broadcasted_iota(jnp.int32, (devices, count), 0) * local_terms
    owned = ((picks >= first) & (picks < first + local_terms)).astype(F32)
    before = lax.broadcasted_iota(jnp.int32, (count, count), 0)
    after = lax.broadcasted_iota(jnp.int32, (count, count), 1)
    rank = jnp.dot(
        owned.astype(BF16),
        (before < after).astype(F32).astype(BF16),
        preferred_element_type=F32,
    )
    return owned, rank


def pack_kernel(place, picks, design, packed, most, held, where, sems):
    devices = packed.shape[0]
    local_terms = design.shape[1]
    chunk = local_terms // CHUNKS

    def part(step):
        columns = pl.ds(step * chunk, chunk)
        return pltpu.make_async_copy(
            design.at[:, columns], held.at[:, columns], sems.at[step]
        )

    for step in range(CHUNKS):
        part(step).start()
    line = as_line(picks)
    owned, rank = owners(line, devices, local_terms)
    counts = jnp.sum(owned, axis=1, keepdims=True)
    most[0] = jnp.max(counts).astype(jnp.int32)
    me = lax.broadcasted_iota(jnp.int32, owned.shape, 0) == place[0]
    mine = jnp.where(me, owned, 0.0)
    slot = jnp.sum(mine * rank, axis=0, keepdims=True)
    slot = slot - (place[1] * SLOTS).astype(F32)
    slot = jnp.where(jnp.sum(mine, axis=0, keepdims=True) > 0.0, slot, -1.0)
    slots = lax.broadcasted_iota(jnp.int32, (SLOTS, slot.shape[1]), 0).astype(F32)
    inner = (line - place[0] * local_terms + 1).astype(F32)
    inner = jnp.where(slots == slot, inner, 0.0)
    where[...] = jnp.sum(inner, axis=1, keepdims=True).astype(jnp.int32) - 1
    total = jnp.zeros((SLOTS, design.shape[0]), F32)
    for step in range(CHUNKS):
        columns = lax.broadcasted_iota(jnp.int32, (SLOTS, chunk), 1) + step * chunk
        chosen = (columns == where[...]).astype(F32).astype(BF16)
        part(step).wait()
        total = total + lax.dot_general(
            chosen,
            held[:, step * chunk : (step + 1) * chunk],
            (((1,), (1,)), ((), ())),
            preferred_element_type=F32,
        )
    value = total.astype(BF16)
    for partner in range(devices):
        packed[partner] = value


def pack(place, picks, design, devices):
    rows = design.shape[0]
    return call(
        pack_kernel,
        "pack",
        (
            jax.ShapeDtypeStruct((devices, SLOTS, rows), BF16),
            jax.ShapeDtypeStruct((1,), jnp.int32),
        ),
        [SCALAR, WHOLE, pl.BlockSpec(memory_space=pltpu.HBM)],
        (WHOLE, SCALAR),
        [
            pltpu.VMEM(design.shape, design.dtype),
            pltpu.VMEM((SLOTS, 1), jnp.int32),
            pltpu.SemaphoreType.DMA((CHUNKS,)),
        ],
    )(place, picks, design)


def gram_kernel(local_terms, devices, own, has_prior, place, order, slots, other, *refs):
    prior = refs[0] if has_prior else None
    basis, sums = refs[has_prior : has_prior + 2]
    if own:
        moved = refs[-1]
        owned, rank = owners(as_line(order), devices, local_terms)
        first = lax.broadcasted_iota(jnp.int32, owned.shape, 0).astype(F32) * SLOTS
        slot = jnp.sum(owned * rank, axis=0, keepdims=True)
        slot = slot - (place[1] * SLOTS).astype(F32)
        target = slot + jnp.sum(owned * first, axis=0, keepdims=True)
        target = jnp.where((slot >= 0.0) & (slot < SLOTS), target, -1.0)
        lines = lax.broadcasted_iota(jnp.int32, moved.shape, 0).astype(F32)
        moved[...] = (lines == target).astype(F32).astype(BF16)
    else:
        moved = order
    count = moved.shape[1]
    columns = lax.dot_general(
        moved[...], slots[...], (((0,), (0,)), ((), ())), preferred_element_type=F32
    )
    if has_prior:
        columns = columns + prior[...].astype(F32)
    basis[...] = columns.astype(BF16)

    def fill(side):
        row = 0
        for top, bottom, start, stop in HALVES[side]:
            strip = lax.dot_general(
                basis[top:bottom],
                basis[start:stop],
                (((1,), (1,)), ((), ())),
                preferred_element_type=F32,
            )
            for j in range(0, stop - start, BLOCK):
                after = row + bottom - top
                piece = strip[:, j : j + BLOCK]
                sums[row:after, :] = piece if own else piece + other[row:after, :]
                row = after
        if not own:
            sums[row:, :] = other[row:, :]
            return
        resp = other.shape[0]
        inner = split_dot(other[...], basis[...], ((1,), (1,)))
        for j in range(0, count, BLOCK):
            sums[row : row + resp, :] = inner[:, j : j + BLOCK]
            row += resp
        sums[row:, :] = jnp.zeros((sums.shape[0] - row, LANES), F32)

    for side in range(2):
        pl.when(place[2] == side)(functools.partial(fill, side))


def gram(place, order, slots, other, local_terms, half, own, prior=None):
    devices, _, rows = slots.shape
    count = order.size if own else order.shape[1]
    extra = () if prior is None else (prior,)
    operands = (place, order, slots.reshape(-1, rows), other, *extra)
    shapes = (
        jax.ShapeDtypeStruct((count, rows), BF16),
        jax.ShapeDtypeStruct((half, LANES), F32),
        jax.ShapeDtypeStruct((devices * SLOTS, count), BF16),
    )
    shapes = shapes if own else shapes[:2]
    return call(
        functools.partial(gram_kernel, local_terms, devices, own, prior is not None),
        "gram",
        shapes,
        [SCALAR] + [WHOLE] * (len(operands) - 1),
        (WHOLE,) * len(shapes),
        cost_estimate=pl.CostEstimate(
            flops=2 * count * rows * (devices * SLOTS + count),
            bytes_accessed=2 * count * rows,
            transcendentals=0,
        ),
    )(*operands)


def split(value):
    parts = []
    for _ in range(3):
        parts.append(value.astype(BF16).astype(F32))
        value = value - parts[-1]
    return parts


def left_parts(value, axis):
    a, b, c = split(value)
    return jnp.concatenate([a, a, a, b, b, c], axis=axis).astype(BF16)


def right_parts(value):
    a, b, c = split(value)
    return jnp.concatenate([a, b, c, a, b, a], axis=0).astype(BF16)


def dot_parts(left, right, axis=1):
    return lax.dot_general(
        left, right, (((axis,), (0,)), ((), ())), preferred_element_type=F32
    )


def dot(left, right):
    return dot_parts(left_parts(left, 1), right_parts(right))


def split_dot(left, right, dims):
    rows = left.shape[0]
    out = lax.dot_general(
        jnp.concatenate(split(left), axis=0).astype(BF16),
        right,
        (dims, ((), ())),
        preferred_element_type=F32,
    )
    return out[2 * rows :] + out[rows : 2 * rows] + out[:rows]


def total_kernel(pieces, totals):
    total = jnp.sum(pieces[...], axis=0).astype(totals.dtype)
    totals[...] = jnp.broadcast_to(total, totals.shape)


def totals(pieces, sent):
    shape = jax.ShapeDtypeStruct(pieces.shape, sent)
    return call(total_kernel, "totals", shape, [WHOLE], WHOLE)(pieces)


def spread(piece):
    return jnp.broadcast_to(piece, (SUB, LANES))


def across(group, lane):
    index = jnp.full((SUB, LANES), lane, jnp.int32)
    return jnp.take_along_axis(group, index, axis=1, mode="promise_in_bounds")


def invert_small(columns, sub):
    for i in range(SUB):
        pivot = 1.0 / spread(columns[i][i : i + 1, :])
        column, here = columns[i], sub == i
        after = []
        for j in range(SUB):
            if j == i:
                after.append(jnp.where(here, pivot, -column * pivot))
            else:
                factor = spread(columns[j][i : i + 1, :]) * pivot
                after.append(jnp.where(here, factor, columns[j] - column * factor))
        columns = after
    return columns


def invert_block(groups):
    lane = lax.broadcasted_iota(jnp.int32, (SUB, LANES), 1)
    sub = lax.broadcasted_iota(jnp.int32, (SUB, LANES), 0)
    groups = list(groups)
    count = len(groups)
    for k in range(count):
        first = SUB * k
        mine = groups[k]
        turned = left_parts(jnp.where(lane < first, -mine, mine), 0)
        small = invert_small([across(mine, first + j) for j in range(SUB)], sub)
        inside = (lane >= first) & (lane < first + SUB)
        unit = jnp.where(lane - first == sub, 1.0, 0.0)
        mine = jnp.where(inside, unit, mine)
        terms = [small[j] * spread(mine[j : j + 1, :]) for j in range(SUB)]
        while len(terms) > 1:
            terms = [terms[i] + terms[i + 1] for i in range(0, len(terms), 2)]
        top = terms[0]
        change = dot_parts(turned, right_parts(top), 0)
        for g in range(count):
            new = jnp.where(inside, 0.0, groups[g])
            if g == k + 1:
                for j in range(SUB):
                    row = spread(top[j : j + 1, :])
                    new = new - across(groups[g], first + j) * row
            else:
                new = new - change[SUB * g : SUB * (g + 1), :]
            groups[g] = new
        groups[k] = top
    return groups


def groups_of(block):
    return [block[SUB * g : SUB * (g + 1), :] for g in range(BLOCK // SUB)]


def first_kernel(sums, inverse):
    for g, group in enumerate(invert_block(groups_of(sums[:BLOCK, :]))):
        inverse[SUB * g : SUB * (g + 1), :] = group


def first_inverse(sums):
    return call(
        first_kernel,
        "first_inverse",
        jax.ShapeDtypeStruct((BLOCK, BLOCK), F32),
        [WHOLE],
        WHOLE,
        cost_estimate=pl.CostEstimate(
            flops=2 * 10**9, bytes_accessed=10**5, transcendentals=0
        ),
    )(sums)


def finish_kernel(scale, place, *refs):
    mine, other, known_inverse, responses, basis, design, residual, pieces = refs[:8]
    work, inverse, coef = refs[8:]
    count = basis.shape[0]
    resp = responses.shape[0]
    blocks = count // BLOCK
    core = place[2]

    def place_side(side, source):
        row = 0
        for top, bottom, start, stop in HALVES[side]:
            for j in range(start, stop, BLOCK):
                after = row + bottom - top
                work[top:bottom, j : j + BLOCK] = source[row:after, :]
                row = after

    for side in range(2):
        pl.when(core == side)(functools.partial(place_side, side, mine))
        pl.when(core != side)(functools.partial(place_side, side, other))
    for i in range(blocks):
        at = pl.ds(INNER + i * resp, resp)
        tall = [mine[at, :] + other[at, :], jnp.zeros((BLOCK - resp, BLOCK), F32)]
        work[i * BLOCK : (i + 1) * BLOCK, count:] = jnp.concatenate(tall, axis=0).T

    def eliminate(k):
        start, stop = k * BLOCK, (k + 1) * BLOCK
        right = work[start:stop, stop:]
        lead = dot(inverse[...], right)
        if stop < count:
            turned = right[:, : count - stop].T
            work[stop:, stop:] = work[stop:, stop:] - dot(turned, lead)
        work[start:stop, stop:] = lead

    def step(k, carry):
        start = pl.multiple_of(k * BLOCK, BLOCK)
        groups = [
            work[pl.ds(pl.multiple_of(start + SUB * g, SUB), SUB), pl.ds(start, BLOCK)]
            for g in range(BLOCK // SUB)
        ]
        for g, group in enumerate(invert_block(groups)):
            inverse[SUB * g : SUB * (g + 1), :] = group
        for known in range(1, blocks):
            pl.when(k == known)(functools.partial(eliminate, known))
        return carry

    inverse[...] = known_inverse[...]
    eliminate(0)
    lax.fori_loop(1, blocks, step, 0)
    coef[count - BLOCK :, :] = work[count - BLOCK :, count:]
    for k in reversed(range(blocks - 1)):
        start, stop = k * BLOCK, (k + 1) * BLOCK
        coef[start:stop, :] = work[start:stop, count:] - dot(
            work[start:stop, stop:count], coef[stop:, :]
        )
    fitted = split_dot(coef[...].T[:resp, :], basis[...], ((1,), (0,)))
    left = responses[...] - fitted
    residual[...] = left
    rounded = left.astype(BF16)
    tiles = design.shape[1] // LANES
    for tile in range(0, tiles, 2):
        part = design[:, tile * LANES : (tile + 2) * LANES]
        both = jnp.dot(rounded, part, preferred_element_type=F32) * scale
        pieces[tile] = both[:, :LANES]
        pieces[tile + 1] = both[:, LANES:]
    pieces[tiles:] = jnp.zeros((pieces.shape[0] - tiles, resp, LANES), F32)


def finish(place, mine, other, inverse, responses, basis, design, pieces, scale):
    resp, rows = responses.shape
    count = basis.shape[0]
    return call(
        functools.partial(finish_kernel, scale),
        "finish",
        (
            jax.ShapeDtypeStruct((resp, rows), F32),
            jax.ShapeDtypeStruct((pieces, resp, LANES), F32),
        ),
        [SCALAR] + [WHOLE] * 6,
        (WHOLE, WHOLE),
        [
            pltpu.VMEM((count, count + LANES), F32),
            pltpu.VMEM((BLOCK, BLOCK), F32),
            pltpu.VMEM((count, LANES), F32),
        ],
    )(place, mine, other, inverse, responses, basis, design)


def summed_everywhere(pieces, axis, groups=None, sent=F32):
    return exchange(totals(exchange(pieces, axis, groups), sent), axis, groups)


def local(design, responses, picks):
    run_devices, term_devices = lax.axis_size("runs"), lax.axis_size("terms")
    resp, local_rows = responses.shape
    local_terms = design.shape[1]
    chips = run_devices // 2
    core = lax.axis_index("runs") % 2
    swap = [(i, i ^ 1) for i in range(run_devices)]
    sides = [list(range(side, run_devices, 2)) for side in range(2)]
    count = picks.size
    half = (4 + 2) * BLOCK

    def fetch(turn):
        where = jnp.stack([lax.axis_index("terms"), jnp.int32(turn), core])
        packed, most = pack(where, picks, design, term_devices)
        return where, exchange(packed, "terms"), most

    def grams(where, slots, prior=(None, None)):
        partner_slots = lax.ppermute(slots, "runs", swap)
        basis, sums, order = gram(
            where, picks, slots, responses, local_terms, half, True, prior[0]
        )
        partner_basis, sums = gram(
            where, order, partner_slots, sums, local_terms, half, False, prior[1]
        )
        return basis, partner_basis, sums

    at, slots, most = fetch(0)
    state = grams(at, slots)

    def another(carry):
        turn, basis, partner_basis, _ = carry
        where, more, _ = fetch(turn)
        return turn + 1, *grams(where, more, (basis, partner_basis))

    _, basis, _, sums = lax.while_loop(
        lambda carry: carry[0] * SLOTS < most[0], another, (jnp.int32(1), *state)
    )

    mine = summed_everywhere(sums.reshape(chips, -1, LANES), "runs", sides)
    mine = mine.reshape(half, LANES)
    other = lax.ppermute(mine, "runs", swap)
    inverse = first_inverse(mine)

    scale = float(local_rows * run_devices) ** -0.5
    residual, pieces = finish(
        at, mine, other, inverse, responses, basis, design, run_devices, scale
    )
    gathered = summed_everywhere(pieces, "runs", sent=BF16)[: local_terms // LANES]
    correlations = gathered.transpose(1, 0, 2).reshape(resp, -1).astype(F32)
    return (residual, correlations)


def solution(mesh):
    placed = (P("runs", "terms"), P(None, "runs"), P())
    return jax.shard_map(
        local,
        mesh=mesh,
        in_specs=placed,
        out_specs=(P(None, "runs"), P(None, "terms")),
        check_vma=False,
    )
```

```python
import functools

import jax
import jax.numpy as jnp
from jax import lax
from jax.experimental import pallas as pl
from jax.experimental.pallas import tpu as pltpu
from jax.sharding import PartitionSpec as P

LANES = 128
SUB = 8
BLOCK = 128
SLOTS = 96
CHUNKS = 2
HALVES = (
    ((0, 128, 0, 512), (128, 256, 128, 256), (128, 192, 256, 384)),
    (
        (0, 128, 0, 128),
        (192, 256, 256, 384),
        (128, 256, 384, 512),
        (256, 384, 256, 512),
        (384, 512, 384, 512),
    ),
)
INNER = 704
F32 = jnp.float32
BF16 = jnp.bfloat16


def call(kernel, name, out_shape, in_specs, out_specs, scratch=(), vmem=32, **more):
    return pl.pallas_call(
        kernel,
        out_shape=out_shape,
        in_specs=in_specs,
        out_specs=out_specs,
        scratch_shapes=scratch,
        compiler_params=pltpu.CompilerParams(vmem_limit_bytes=vmem * 2**20),
        name=name,
        **more,
    )


WHOLE = pl.BlockSpec(memory_space=pltpu.VMEM)
SCALAR = pl.BlockSpec(memory_space=pltpu.SMEM)


def exchange(pieces, axis, groups=None):
    return lax.all_to_all(pieces, axis, 0, 0, axis_index_groups=groups)


def as_line(picks):
    return jnp.concatenate([picks[i : i + 1, :] for i in range(picks.shape[0])], axis=1)


def owners(picks, devices, local_terms):
    count = picks.shape[1]
    first = lax.broadcasted_iota(jnp.int32, (devices, count), 0) * local_terms
    owned = ((picks >= first) & (picks < first + local_terms)).astype(F32)
    before = lax.broadcasted_iota(jnp.int32, (count, count), 0)
    after = lax.broadcasted_iota(jnp.int32, (count, count), 1)
    rank = jnp.dot(
        owned.astype(BF16),
        (before < after).astype(F32).astype(BF16),
        preferred_element_type=F32,
    )
    return owned, rank


def pack_kernel(place, picks, design, packed, most, held, where, sems):
    devices = packed.shape[0]
    local_terms = design.shape[1]
    chunk = local_terms // CHUNKS

    def part(step):
        columns = pl.ds(step * chunk, chunk)
        return pltpu.make_async_copy(
            design.at[:, columns], held.at[:, columns], sems.at[step]
        )

    for step in range(CHUNKS):
        part(step).start()
    line = as_line(picks)
    owned, rank = owners(line, devices, local_terms)
    counts = jnp.sum(owned, axis=1, keepdims=True)
    most[0] = jnp.max(counts).astype(jnp.int32)
    me = lax.broadcasted_iota(jnp.int32, owned.shape, 0) == place[0]
    mine = jnp.where(me, owned, 0.0)
    slot = jnp.sum(mine * rank, axis=0, keepdims=True)
    slot = slot - (place[1] * SLOTS).astype(F32)
    slot = jnp.where(jnp.sum(mine, axis=0, keepdims=True) > 0.0, slot, -1.0)
    slots = lax.broadcasted_iota(jnp.int32, (SLOTS, slot.shape[1]), 0).astype(F32)
    inner = (line - place[0] * local_terms + 1).astype(F32)
    inner = jnp.where(slots == slot, inner, 0.0)
    where[...] = jnp.sum(inner, axis=1, keepdims=True).astype(jnp.int32) - 1
    total = jnp.zeros((SLOTS, design.shape[0]), F32)
    for step in range(CHUNKS):
        columns = lax.broadcasted_iota(jnp.int32, (SLOTS, chunk), 1) + step * chunk
        chosen = (columns == where[...]).astype(F32).astype(BF16)
        part(step).wait()
        total = total + lax.dot_general(
            chosen,
            held[:, step * chunk : (step + 1) * chunk],
            (((1,), (1,)), ((), ())),
            preferred_element_type=F32,
        )
    value = total.astype(BF16)
    for partner in range(devices):
        packed[partner] = value


def pack(place, picks, design, devices):
    rows = design.shape[0]
    return call(
        pack_kernel,
        "pack",
        (
            jax.ShapeDtypeStruct((devices, SLOTS, rows), BF16),
            jax.ShapeDtypeStruct((1,), jnp.int32),
        ),
        [SCALAR, WHOLE, pl.BlockSpec(memory_space=pltpu.HBM)],
        (WHOLE, SCALAR),
        [
            pltpu.VMEM(design.shape, design.dtype),
            pltpu.VMEM((SLOTS, 1), jnp.int32),
            pltpu.SemaphoreType.DMA((CHUNKS,)),
        ],
    )(place, picks, design)


def unpack_kernel(local_terms, devices, place, picks, slots, *refs):
    owned, rank = owners(as_line(picks), devices, local_terms)
    first = lax.broadcasted_iota(jnp.int32, owned.shape, 0).astype(F32) * SLOTS
    slot = jnp.sum(owned * rank, axis=0, keepdims=True)
    slot = slot - (place[1] * SLOTS).astype(F32)
    target = slot + jnp.sum(owned * first, axis=0, keepdims=True)
    target = jnp.where((slot >= 0.0) & (slot < SLOTS), target, -1.0)
    shape = (slots.shape[0], target.shape[1])
    lines = lax.broadcasted_iota(jnp.int32, shape, 0).astype(F32)
    moved = (lines == target).astype(F32).astype(BF16)
    columns = lax.dot_general(
        moved, slots[...], (((0,), (0,)), ((), ())), preferred_element_type=F32
    )
    for earlier in refs[:-1]:
        columns = columns + earlier[...].astype(F32)
    refs[-1][...] = columns.astype(BF16)


def unpack(place, picks, slots, local_terms, *earlier):
    devices, _, rows = slots.shape
    operands = (place, picks, slots.reshape(-1, rows), *earlier)
    return call(
        functools.partial(unpack_kernel, local_terms, devices),
        "unpack",
        jax.ShapeDtypeStruct((picks.size, rows), BF16),
        [SCALAR] + [WHOLE] * (len(operands) - 1),
        WHOLE,
    )(*operands)


def gram_kernel(place, basis, other, sums):
    own = other.shape[0] != sums.shape[0]
    count = basis.shape[0]

    def fill(side):
        row = 0
        for top, bottom, start, stop in HALVES[side]:
            strip = lax.dot_general(
                basis[top:bottom],
                basis[start:stop],
                (((1,), (1,)), ((), ())),
                preferred_element_type=F32,
            )
            for j in range(0, stop - start, BLOCK):
                after = row + bottom - top
                piece = strip[:, j : j + BLOCK]
                sums[row:after, :] = piece if own else piece + other[row:after, :]
                row = after
        if not own:
            sums[row:, :] = other[row:, :]
            return
        resp = other.shape[0]
        inner = split_dot(other[...], basis[...], ((1,), (1,)))
        for j in range(0, count, BLOCK):
            sums[row : row + resp, :] = inner[:, j : j + BLOCK]
            row += resp
        sums[row:, :] = jnp.zeros((sums.shape[0] - row, LANES), F32)

    for side in range(2):
        pl.when(place[2] == side)(functools.partial(fill, side))


def gram(place, basis, other, half):
    count, rows = basis.shape
    return call(
        gram_kernel,
        "gram",
        jax.ShapeDtypeStruct((half, LANES), F32),
        [SCALAR, WHOLE, WHOLE],
        WHOLE,
        cost_estimate=pl.CostEstimate(
            flops=2 * count * rows * 1024,
            bytes_accessed=2 * count * rows,
            transcendentals=0,
        ),
    )(place, basis, other)


def split(value):
    parts = []
    for _ in range(3):
        parts.append(value.astype(BF16).astype(F32))
        value = value - parts[-1]
    return parts


def left_parts(value, axis):
    a, b, c = split(value)
    return jnp.concatenate([a, a, a, b, b, c], axis=axis).astype(BF16)


def right_parts(value):
    a, b, c = split(value)
    return jnp.concatenate([a, b, c, a, b, a], axis=0).astype(BF16)


def dot_parts(left, right, axis=1):
    return lax.dot_general(
        left, right, (((axis,), (0,)), ((), ())), preferred_element_type=F32
    )


def dot(left, right):
    return dot_parts(left_parts(left, 1), right_parts(right))


def split_dot(left, right, dims):
    rows = left.shape[0]
    out = lax.dot_general(
        jnp.concatenate(split(left), axis=0).astype(BF16),
        right,
        (dims, ((), ())),
        preferred_element_type=F32,
    )
    return out[2 * rows :] + out[rows : 2 * rows] + out[:rows]


def total_kernel(pieces, totals):
    total = jnp.sum(pieces[...], axis=0).astype(totals.dtype)
    totals[...] = jnp.broadcast_to(total, totals.shape)


def totals(pieces, sent):
    shape = jax.ShapeDtypeStruct(pieces.shape, sent)
    return call(total_kernel, "totals", shape, [WHOLE], WHOLE)(pieces)


def spread(piece):
    return jnp.broadcast_to(piece, (SUB, LANES))


def across(group, lane):
    index = jnp.full((SUB, LANES), lane, jnp.int32)
    return jnp.take_along_axis(group, index, axis=1, mode="promise_in_bounds")


def invert_small(columns, sub):
    for i in range(SUB):
        pivot = 1.0 / spread(columns[i][i : i + 1, :])
        column, here = columns[i], sub == i
        after = []
        for j in range(SUB):
            if j == i:
                after.append(jnp.where(here, pivot, -column * pivot))
            else:
                factor = spread(columns[j][i : i + 1, :]) * pivot
                after.append(jnp.where(here, factor, columns[j] - column * factor))
        columns = after
    return columns


def invert_block(groups):
    lane = lax.broadcasted_iota(jnp.int32, (SUB, LANES), 1)
    sub = lax.broadcasted_iota(jnp.int32, (SUB, LANES), 0)
    groups = list(groups)
    count = len(groups)
    for k in range(count):
        first = SUB * k
        mine = groups[k]
        turned = left_parts(jnp.where(lane < first, -mine, mine), 0)
        small = invert_small([across(mine, first + j) for j in range(SUB)], sub)
        inside = (lane >= first) & (lane < first + SUB)
        unit = jnp.where(lane - first == sub, 1.0, 0.0)
        mine = jnp.where(inside, unit, mine)
        terms = [small[j] * spread(mine[j : j + 1, :]) for j in range(SUB)]
        while len(terms) > 1:
            terms = [terms[i] + terms[i + 1] for i in range(0, len(terms), 2)]
        top = terms[0]
        change = dot_parts(turned, right_parts(top), 0)
        for g in range(count):
            new = jnp.where(inside, 0.0, groups[g])
            if g == k + 1:
                for j in range(SUB):
                    row = spread(top[j : j + 1, :])
                    new = new - across(groups[g], first + j) * row
            else:
                new = new - change[SUB * g : SUB * (g + 1), :]
            groups[g] = new
        groups[k] = top
    return groups


def groups_of(block):
    return [block[SUB * g : SUB * (g + 1), :] for g in range(BLOCK // SUB)]


def first_kernel(sums, inverse):
    for g, group in enumerate(invert_block(groups_of(sums[:BLOCK, :]))):
        inverse[SUB * g : SUB * (g + 1), :] = group


def first_inverse(sums):
    return call(
        first_kernel,
        "first_inverse",
        jax.ShapeDtypeStruct((BLOCK, BLOCK), F32),
        [WHOLE],
        WHOLE,
        cost_estimate=pl.CostEstimate(
            flops=2 * 10**9, bytes_accessed=10**5, transcendentals=0
        ),
    )(sums)


def finish_kernel(scale, place, *refs):
    mine, other, known_inverse, responses, basis, design, residual, pieces = refs[:8]
    work, inverse, coef = refs[8:]
    count = basis.shape[0]
    resp = responses.shape[0]
    blocks = count // BLOCK
    core = place[2]

    def place_side(side, source):
        row = 0
        for top, bottom, start, stop in HALVES[side]:
            for j in range(start, stop, BLOCK):
                after = row + bottom - top
                work[top:bottom, j : j + BLOCK] = source[row:after, :]
                row = after

    for side in range(2):
        pl.when(core == side)(functools.partial(place_side, side, mine))
        pl.when(core != side)(functools.partial(place_side, side, other))
    for i in range(blocks):
        at = pl.ds(INNER + i * resp, resp)
        tall = [mine[at, :] + other[at, :], jnp.zeros((BLOCK - resp, BLOCK), F32)]
        work[i * BLOCK : (i + 1) * BLOCK, count:] = jnp.concatenate(tall, axis=0).T

    def eliminate(k):
        start, stop = k * BLOCK, (k + 1) * BLOCK
        right = work[start:stop, stop:]
        lead = dot(inverse[...], right)
        if stop < count:
            turned = right[:, : count - stop].T
            work[stop:, stop:] = work[stop:, stop:] - dot(turned, lead)
        work[start:stop, stop:] = lead

    def step(k, carry):
        start = pl.multiple_of(k * BLOCK, BLOCK)
        groups = [
            work[pl.ds(pl.multiple_of(start + SUB * g, SUB), SUB), pl.ds(start, BLOCK)]
            for g in range(BLOCK // SUB)
        ]
        for g, group in enumerate(invert_block(groups)):
            inverse[SUB * g : SUB * (g + 1), :] = group
        for known in range(1, blocks):
            pl.when(k == known)(functools.partial(eliminate, known))
        return carry

    inverse[...] = known_inverse[...]
    eliminate(0)
    lax.fori_loop(1, blocks, step, 0)
    coef[count - BLOCK :, :] = work[count - BLOCK :, count:]
    for k in reversed(range(blocks - 1)):
        start, stop = k * BLOCK, (k + 1) * BLOCK
        coef[start:stop, :] = work[start:stop, count:] - dot(
            work[start:stop, stop:count], coef[stop:, :]
        )
    fitted = split_dot(coef[...].T[:resp, :], basis[...], ((1,), (0,)))
    left = responses[...] - fitted
    residual[...] = left
    rounded = left.astype(BF16)
    tiles = design.shape[1] // LANES
    for tile in range(0, tiles, 2):
        part = design[:, tile * LANES : (tile + 2) * LANES]
        both = jnp.dot(rounded, part, preferred_element_type=F32) * scale
        pieces[tile] = both[:, :LANES]
        pieces[tile + 1] = both[:, LANES:]
    pieces[tiles:] = jnp.zeros((pieces.shape[0] - tiles, resp, LANES), F32)


def finish(place, mine, other, inverse, responses, basis, design, pieces, scale):
    resp, rows = responses.shape
    count = basis.shape[0]
    return call(
        functools.partial(finish_kernel, scale),
        "finish",
        (
            jax.ShapeDtypeStruct((resp, rows), F32),
            jax.ShapeDtypeStruct((pieces, resp, LANES), F32),
        ),
        [SCALAR] + [WHOLE] * 6,
        (WHOLE, WHOLE),
        [
            pltpu.VMEM((count, count + LANES), F32),
            pltpu.VMEM((BLOCK, BLOCK), F32),
            pltpu.VMEM((count, LANES), F32),
        ],
    )(place, mine, other, inverse, responses, basis, design)


def summed_everywhere(pieces, axis, groups=None, sent=F32):
    return exchange(totals(exchange(pieces, axis, groups), sent), axis, groups)


def local(design, responses, picks):
    run_devices, term_devices = lax.axis_size("runs"), lax.axis_size("terms")
    resp, local_rows = responses.shape
    local_terms = design.shape[1]
    chips = run_devices // 2
    core = lax.axis_index("runs") % 2
    swap = [(i, i ^ 1) for i in range(run_devices)]
    sides = [list(range(side, run_devices, 2)) for side in range(2)]
    count = picks.size
    half = (4 + 2) * BLOCK

    def fetch(turn):
        where = jnp.stack([lax.axis_index("terms"), jnp.int32(turn), core])
        packed, most = pack(where, picks, design, term_devices)
        return where, exchange(packed, "terms"), most

    at, slots, most = fetch(0)

    def another(carry):
        turn, basis = carry
        where, more, _ = fetch(turn)
        return turn + 1, unpack(where, picks, more, local_terms, basis)

    _, basis = lax.while_loop(
        lambda carry: carry[0] * SLOTS < most[0],
        another,
        (jnp.int32(1), unpack(at, picks, slots, local_terms)),
    )

    partner = lax.ppermute(basis, "runs", swap)
    sums = gram(at, partner, gram(at, basis, responses, half), half)

    mine = summed_everywhere(sums.reshape(chips, -1, LANES), "runs", sides)
    mine = mine.reshape(half, LANES)
    other = lax.ppermute(mine, "runs", swap)
    inverse = first_inverse(mine)

    scale = float(local_rows * run_devices) ** -0.5
    residual, pieces = finish(
        at, mine, other, inverse, responses, basis, design, run_devices, scale
    )
    gathered = summed_everywhere(pieces, "runs", sent=BF16)[: local_terms // LANES]
    correlations = gathered.transpose(1, 0, 2).reshape(resp, -1).astype(F32)
    return (residual, correlations)


def solution(mesh):
    placed = (P("runs", "terms"), P(None, "runs"), P())
    return jax.shard_map(
        local,
        mesh=mesh,
        in_specs=placed,
        out_specs=(P(None, "runs"), P(None, "terms")),
        check_vma=False,
    )
```

```python
import functools

import jax
import jax.numpy as jnp
from jax import lax
from jax.experimental import pallas as pl
from jax.experimental.pallas import tpu as pltpu
from jax.sharding import PartitionSpec as P

LANES = 128
SUB = 8
BLOCK = 128
SLOTS = 96
CHUNKS = 2
HALVES = (
    ((0, 128, 0, 512), (128, 256, 128, 256), (128, 192, 256, 384)),
    (
        (0, 128, 0, 128),
        (192, 256, 256, 384),
        (128, 256, 384, 512),
        (256, 384, 256, 512),
        (384, 512, 384, 512),
    ),
)
INNER = 704
F32 = jnp.float32
BF16 = jnp.bfloat16


def call(kernel, name, out_shape, in_specs, out_specs, scratch=(), vmem=32, **more):
    return pl.pallas_call(
        kernel,
        out_shape=out_shape,
        in_specs=in_specs,
        out_specs=out_specs,
        scratch_shapes=scratch,
        compiler_params=pltpu.CompilerParams(vmem_limit_bytes=vmem * 2**20),
        name=name,
        **more,
    )


WHOLE = pl.BlockSpec(memory_space=pltpu.VMEM)
SCALAR = pl.BlockSpec(memory_space=pltpu.SMEM)


def exchange(pieces, axis, groups=None):
    return lax.all_to_all(pieces, axis, 0, 0, axis_index_groups=groups)


def as_line(picks):
    return jnp.concatenate([picks[i : i + 1, :] for i in range(picks.shape[0])], axis=1)


def owners(picks, devices, local_terms):
    count = picks.shape[1]
    first = lax.broadcasted_iota(jnp.int32, (devices, count), 0) * local_terms
    owned = ((picks >= first) & (picks < first + local_terms)).astype(F32)
    before = lax.broadcasted_iota(jnp.int32, (count, count), 0)
    after = lax.broadcasted_iota(jnp.int32, (count, count), 1)
    rank = jnp.dot(
        owned.astype(BF16),
        (before < after).astype(F32).astype(BF16),
        preferred_element_type=F32,
    )
    return owned, rank


def pack_kernel(place, picks, design, packed, most, held, where, sems):
    devices = packed.shape[0]
    local_terms = design.shape[1]
    chunk = local_terms // CHUNKS

    def part(step):
        columns = pl.ds(step * chunk, chunk)
        return pltpu.make_async_copy(
            design.at[:, columns], held.at[:, columns], sems.at[step]
        )

    for step in range(CHUNKS):
        part(step).start()
    line = as_line(picks)
    owned, rank = owners(line, devices, local_terms)
    counts = jnp.sum(owned, axis=1, keepdims=True)
    most[0] = jnp.max(counts).astype(jnp.int32)
    me = lax.broadcasted_iota(jnp.int32, owned.shape, 0) == place[0]
    mine = jnp.where(me, owned, 0.0)
    slot = jnp.sum(mine * rank, axis=0, keepdims=True)
    slot = slot - (place[1] * SLOTS).astype(F32)
    slot = jnp.where(jnp.sum(mine, axis=0, keepdims=True) > 0.0, slot, -1.0)
    slots = lax.broadcasted_iota(jnp.int32, (SLOTS, slot.shape[1]), 0).astype(F32)
    inner = (line - place[0] * local_terms + 1).astype(F32)
    inner = jnp.where(slots == slot, inner, 0.0)
    where[...] = jnp.sum(inner, axis=1, keepdims=True).astype(jnp.int32) - 1
    total = jnp.zeros((SLOTS, design.shape[0]), F32)
    for step in range(CHUNKS):
        columns = lax.broadcasted_iota(jnp.int32, (SLOTS, chunk), 1) + step * chunk
        chosen = (columns == where[...]).astype(F32).astype(BF16)
        part(step).wait()
        total = total + lax.dot_general(
            chosen,
            held[:, step * chunk : (step + 1) * chunk],
            (((1,), (1,)), ((), ())),
            preferred_element_type=F32,
        )
    value = total.astype(BF16)
    for partner in range(devices):
        packed[partner] = value


def pack(place, picks, design, devices):
    rows = design.shape[0]
    return call(
        pack_kernel,
        "pack",
        (
            jax.ShapeDtypeStruct((devices, SLOTS, rows), BF16),
            jax.ShapeDtypeStruct((1,), jnp.int32),
        ),
        [SCALAR, WHOLE, pl.BlockSpec(memory_space=pltpu.HBM)],
        (WHOLE, SCALAR),
        [
            pltpu.VMEM(design.shape, design.dtype),
            pltpu.VMEM((SLOTS, 1), jnp.int32),
            pltpu.SemaphoreType.DMA((CHUNKS,)),
        ],
    )(place, picks, design)


def unpack_kernel(local_terms, devices, place, picks, slots, *refs):
    owned, rank = owners(as_line(picks), devices, local_terms)
    first = lax.broadcasted_iota(jnp.int32, owned.shape, 0).astype(F32) * SLOTS
    slot = jnp.sum(owned * rank, axis=0, keepdims=True)
    slot = slot - (place[1] * SLOTS).astype(F32)
    target = slot + jnp.sum(owned * first, axis=0, keepdims=True)
    target = jnp.where((slot >= 0.0) & (slot < SLOTS), target, -1.0)
    shape = (slots.shape[0], target.shape[1])
    lines = lax.broadcasted_iota(jnp.int32, shape, 0).astype(F32)
    moved = (lines == target).astype(F32).astype(BF16)
    columns = lax.dot_general(
        moved, slots[...], (((0,), (0,)), ((), ())), preferred_element_type=F32
    )
    for earlier in refs[:-1]:
        columns = columns + earlier[...].astype(F32)
    refs[-1][...] = columns.astype(BF16)


def unpack(place, picks, slots, local_terms, *earlier):
    devices, _, rows = slots.shape
    operands = (place, picks, slots.reshape(-1, rows), *earlier)
    return call(
        functools.partial(unpack_kernel, local_terms, devices),
        "unpack",
        jax.ShapeDtypeStruct((picks.size, rows), BF16),
        [SCALAR] + [WHOLE] * (len(operands) - 1),
        WHOLE,
    )(*operands)


def gram_kernel(place, basis, other, sums):
    own = other.shape[0] != sums.shape[0]
    count = basis.shape[0]

    def fill(side):
        row = 0
        for top, bottom, start, stop in HALVES[side]:
            strip = lax.dot_general(
                basis[top:bottom],
                basis[start:stop],
                (((1,), (1,)), ((), ())),
                preferred_element_type=F32,
            )
            for j in range(0, stop - start, BLOCK):
                after = row + bottom - top
                piece = strip[:, j : j + BLOCK]
                sums[row:after, :] = piece if own else piece + other[row:after, :]
                row = after
        if not own:
            sums[row:, :] = other[row:, :]
            return
        resp = other.shape[0]
        inner = split_dot(other[...], basis[...], ((1,), (1,)))
        for j in range(0, count, BLOCK):
            sums[row : row + resp, :] = inner[:, j : j + BLOCK]
            row += resp
        sums[row:, :] = jnp.zeros((sums.shape[0] - row, LANES), F32)

    for side in range(2):
        pl.when(place[2] == side)(functools.partial(fill, side))


def gram(place, basis, other, half):
    count, rows = basis.shape
    return call(
        gram_kernel,
        "gram",
        jax.ShapeDtypeStruct((half, LANES), F32),
        [SCALAR, WHOLE, WHOLE],
        WHOLE,
        cost_estimate=pl.CostEstimate(
            flops=2 * count * rows * 1024,
            bytes_accessed=2 * count * rows,
            transcendentals=0,
        ),
    )(place, basis, other)


def split(value):
    parts = []
    for _ in range(3):
        parts.append(value.astype(BF16).astype(F32))
        value = value - parts[-1]
    return parts


def left_parts(value, axis):
    a, b, c = split(value)
    return jnp.concatenate([a, a, a, b, b, c], axis=axis).astype(BF16)


def right_parts(value):
    a, b, c = split(value)
    return jnp.concatenate([a, b, c, a, b, a], axis=0).astype(BF16)


def dot_parts(left, right, axis=1):
    return lax.dot_general(
        left, right, (((axis,), (0,)), ((), ())), preferred_element_type=F32
    )


def dot(left, right):
    return dot_parts(left_parts(left, 1), right_parts(right))


def split_dot(left, right, dims):
    rows = left.shape[0]
    out = lax.dot_general(
        jnp.concatenate(split(left), axis=0).astype(BF16),
        right,
        (dims, ((), ())),
        preferred_element_type=F32,
    )
    return out[2 * rows :] + out[rows : 2 * rows] + out[:rows]


def total_kernel(pieces, totals):
    total = jnp.sum(pieces[...], axis=0).astype(totals.dtype)
    totals[...] = jnp.broadcast_to(total, totals.shape)


def totals(pieces, sent):
    shape = jax.ShapeDtypeStruct(pieces.shape, sent)
    return call(total_kernel, "totals", shape, [WHOLE], WHOLE)(pieces)


def spread(piece):
    return jnp.broadcast_to(piece, (SUB, LANES))


def across(group, lane):
    index = jnp.full((SUB, LANES), lane, jnp.int32)
    return jnp.take_along_axis(group, index, axis=1, mode="promise_in_bounds")


def invert_small(columns, sub):
    for i in range(SUB):
        pivot = 1.0 / spread(columns[i][i : i + 1, :])
        column, here = columns[i], sub == i
        after = []
        for j in range(SUB):
            if j == i:
                after.append(jnp.where(here, pivot, -column * pivot))
            else:
                factor = spread(columns[j][i : i + 1, :]) * pivot
                after.append(jnp.where(here, factor, columns[j] - column * factor))
        columns = after
    return columns


def invert_block(groups):
    lane = lax.broadcasted_iota(jnp.int32, (SUB, LANES), 1)
    sub = lax.broadcasted_iota(jnp.int32, (SUB, LANES), 0)
    groups = list(groups)
    count = len(groups)
    for k in range(count):
        first = SUB * k
        mine = groups[k]
        turned = left_parts(jnp.where(lane < first, -mine, mine), 0)
        small = invert_small([across(mine, first + j) for j in range(SUB)], sub)
        inside = (lane >= first) & (lane < first + SUB)
        unit = jnp.where(lane - first == sub, 1.0, 0.0)
        mine = jnp.where(inside, unit, mine)
        terms = [small[j] * spread(mine[j : j + 1, :]) for j in range(SUB)]
        while len(terms) > 1:
            terms = [terms[i] + terms[i + 1] for i in range(0, len(terms), 2)]
        top = terms[0]
        change = dot_parts(turned, right_parts(top), 0)
        for g in range(count):
            new = jnp.where(inside, 0.0, groups[g])
            if g == k + 1:
                for j in range(SUB):
                    row = spread(top[j : j + 1, :])
                    new = new - across(groups[g], first + j) * row
            else:
                new = new - change[SUB * g : SUB * (g + 1), :]
            groups[g] = new
        groups[k] = top
    return groups


def groups_of(block):
    return [block[SUB * g : SUB * (g + 1), :] for g in range(BLOCK // SUB)]


def first_kernel(sums, inverse):
    for g, group in enumerate(invert_block(groups_of(sums[:BLOCK, :]))):
        inverse[SUB * g : SUB * (g + 1), :] = group


def first_inverse(sums):
    return call(
        first_kernel,
        "first_inverse",
        jax.ShapeDtypeStruct((BLOCK, BLOCK), F32),
        [WHOLE],
        WHOLE,
        cost_estimate=pl.CostEstimate(
            flops=2 * 10**9, bytes_accessed=10**5, transcendentals=0
        ),
    )(sums)


def finish_kernel(scale, place, *refs):
    mine, other, known_inverse, responses, basis, design, residual, pieces = refs[:8]
    work, inverse, coef = refs[8:]
    count = basis.shape[0]
    resp = responses.shape[0]
    blocks = count // BLOCK
    core = place[2]

    def place_side(side, source):
        row = 0
        for top, bottom, start, stop in HALVES[side]:
            for j in range(start, stop, BLOCK):
                after = row + bottom - top
                work[top:bottom, j : j + BLOCK] = source[row:after, :]
                row = after

    for side in range(2):
        pl.when(core == side)(functools.partial(place_side, side, mine))
        pl.when(core != side)(functools.partial(place_side, side, other))
    for i in range(blocks):
        at = pl.ds(INNER + i * resp, resp)
        tall = [mine[at, :] + other[at, :], jnp.zeros((BLOCK - resp, BLOCK), F32)]
        work[i * BLOCK : (i + 1) * BLOCK, count:] = jnp.concatenate(tall, axis=0).T

    def eliminate(k):
        start, stop = k * BLOCK, (k + 1) * BLOCK
        right = work[start:stop, stop:]
        lead = dot(inverse[...], right)
        if stop < count:
            turned = right[:, : count - stop].T
            work[stop:, stop:] = work[stop:, stop:] - dot(turned, lead)
        work[start:stop, stop:] = lead

    def step(k, carry):
        start = pl.multiple_of(k * BLOCK, BLOCK)
        groups = [
            work[pl.ds(pl.multiple_of(start + SUB * g, SUB), SUB), pl.ds(start, BLOCK)]
            for g in range(BLOCK // SUB)
        ]
        for g, group in enumerate(invert_block(groups)):
            inverse[SUB * g : SUB * (g + 1), :] = group
        for known in range(1, blocks):
            pl.when(k == known)(functools.partial(eliminate, known))
        return carry

    inverse[...] = known_inverse[...]
    eliminate(0)
    lax.fori_loop(1, blocks, step, 0)
    coef[count - BLOCK :, :] = work[count - BLOCK :, count:]
    for k in reversed(range(blocks - 1)):
        start, stop = k * BLOCK, (k + 1) * BLOCK
        coef[start:stop, :] = work[start:stop, count:] - dot(
            work[start:stop, stop:count], coef[stop:, :]
        )
    fitted = split_dot(coef[...].T[:resp, :], basis[...], ((1,), (0,)))
    left = responses[...] - fitted
    residual[...] = left
    rounded = left.astype(BF16)
    tiles = design.shape[1] // LANES
    for tile in range(0, tiles, 2):
        part = design[:, tile * LANES : (tile + 2) * LANES]
        both = jnp.dot(rounded, part, preferred_element_type=F32) * scale
        pieces[tile] = both[:, :LANES]
        pieces[tile + 1] = both[:, LANES:]
    pieces[tiles:] = jnp.zeros((pieces.shape[0] - tiles, resp, LANES), F32)


def finish(place, mine, other, inverse, responses, basis, design, pieces, scale):
    resp, rows = responses.shape
    count = basis.shape[0]
    return call(
        functools.partial(finish_kernel, scale),
        "finish",
        (
            jax.ShapeDtypeStruct((resp, rows), F32),
            jax.ShapeDtypeStruct((pieces, resp, LANES), F32),
        ),
        [SCALAR] + [WHOLE] * 6,
        (WHOLE, WHOLE),
        [
            pltpu.VMEM((count, count + LANES), F32),
            pltpu.VMEM((BLOCK, BLOCK), F32),
            pltpu.VMEM((count, LANES), F32),
        ],
    )(place, mine, other, inverse, responses, basis, design)


def summed_everywhere(pieces, axis, groups=None, sent=F32):
    return exchange(totals(exchange(pieces, axis, groups), sent), axis, groups)


def local(design, responses, picks):
    run_devices, term_devices = lax.axis_size("runs"), lax.axis_size("terms")
    resp, local_rows = responses.shape
    local_terms = design.shape[1]
    chips = run_devices // 2
    core = lax.axis_index("runs") % 2
    swap = [(i, i ^ 1) for i in range(run_devices)]
    sides = [list(range(side, run_devices, 2)) for side in range(2)]
    count = picks.size
    half = (4 + 2) * BLOCK

    def fetch(turn):
        where = jnp.stack([lax.axis_index("terms"), jnp.int32(turn), core])
        packed, most = pack(where, picks, design, term_devices)
        return where, exchange(packed, "terms"), most

    at, slots, most = fetch(0)
    first, slots = lax.optimization_barrier((jnp.int32(1), slots))

    def another(carry):
        turn, basis = carry
        where, more, _ = fetch(turn)
        return turn + 1, unpack(where, picks, more, local_terms, basis)

    _, basis = lax.while_loop(
        lambda carry: carry[0] * SLOTS < most[0],
        another,
        (first, unpack(at, picks, slots, local_terms)),
    )

    partner = lax.ppermute(basis, "runs", swap)
    sums = gram(at, partner, gram(at, basis, responses, half), half)

    mine = summed_everywhere(sums.reshape(chips, -1, LANES), "runs", sides)
    mine = mine.reshape(half, LANES)
    other = lax.ppermute(mine, "runs", swap)
    inverse = first_inverse(mine)

    scale = float(local_rows * run_devices) ** -0.5
    residual, pieces = finish(
        at, mine, other, inverse, responses, basis, design, run_devices, scale
    )
    gathered = summed_everywhere(pieces, "runs", sent=BF16)[: local_terms // LANES]
    correlations = gathered.transpose(1, 0, 2).reshape(resp, -1).astype(F32)
    return (residual, correlations)


def solution(mesh):
    placed = (P("runs", "terms"), P(None, "runs"), P())
    return jax.shard_map(
        local,
        mesh=mesh,
        in_specs=placed,
        out_specs=(P(None, "runs"), P(None, "terms")),
        check_vma=False,
    )
```

```python
import functools

import jax
import jax.numpy as jnp
from jax import lax
from jax.experimental import pallas as pl
from jax.experimental.pallas import tpu as pltpu
from jax.sharding import PartitionSpec as P

LANES = 128
SUB = 8
BLOCK = 128
SLOTS = 96
CHUNKS = 2
HALVES = (
    ((0, 128, 0, 512), (128, 256, 128, 256), (128, 192, 256, 384)),
    (
        (0, 128, 0, 128),
        (192, 256, 256, 384),
        (128, 256, 384, 512),
        (256, 384, 256, 512),
        (384, 512, 384, 512),
    ),
)
INNER = 704
F32 = jnp.float32
BF16 = jnp.bfloat16


def call(kernel, name, out_shape, in_specs, out_specs, scratch=(), vmem=32, **more):
    return pl.pallas_call(
        kernel,
        out_shape=out_shape,
        in_specs=in_specs,
        out_specs=out_specs,
        scratch_shapes=scratch,
        compiler_params=pltpu.CompilerParams(vmem_limit_bytes=vmem * 2**20),
        name=name,
        **more,
    )


WHOLE = pl.BlockSpec(memory_space=pltpu.VMEM)
SCALAR = pl.BlockSpec(memory_space=pltpu.SMEM)


def exchange(pieces, axis, groups=None):
    return lax.all_to_all(pieces, axis, 0, 0, axis_index_groups=groups)


def as_line(picks):
    return jnp.concatenate([picks[i : i + 1, :] for i in range(picks.shape[0])], axis=1)


def owners(picks, devices, local_terms):
    count = picks.shape[1]
    first = lax.broadcasted_iota(jnp.int32, (devices, count), 0) * local_terms
    owned = ((picks >= first) & (picks < first + local_terms)).astype(F32)
    before = lax.broadcasted_iota(jnp.int32, (count, count), 0)
    after = lax.broadcasted_iota(jnp.int32, (count, count), 1)
    rank = jnp.dot(
        owned.astype(BF16),
        (before < after).astype(F32).astype(BF16),
        preferred_element_type=F32,
    )
    return owned, rank


def pack_kernel(place, picks, design, packed, most, target, held, where, sems):
    devices = packed.shape[0]
    local_terms = design.shape[1]
    chunk = local_terms // CHUNKS

    def part(step):
        columns = pl.ds(step * chunk, chunk)
        return pltpu.make_async_copy(
            design.at[:, columns], held.at[:, columns], sems.at[step]
        )

    for step in range(CHUNKS):
        part(step).start()
    line = as_line(picks)
    owned, rank = owners(line, devices, local_terms)
    counts = jnp.sum(owned, axis=1, keepdims=True)
    most[0] = jnp.max(counts).astype(jnp.int32)
    device = lax.broadcasted_iota(jnp.int32, owned.shape, 0)
    slot = jnp.sum(owned * rank, axis=0, keepdims=True)
    slot = slot - (place[1] * SLOTS).astype(F32)
    start = jnp.sum(owned * device.astype(F32), axis=0, keepdims=True) * SLOTS
    received = jnp.where((slot >= 0.0) & (slot < SLOTS), slot + start, -1.0)
    target[...] = jnp.broadcast_to(received, target.shape)
    mine = jnp.where(device == place[0], owned, 0.0)
    slot = jnp.where(jnp.sum(mine, axis=0, keepdims=True) > 0.0, slot, -1.0)
    slots = lax.broadcasted_iota(jnp.int32, (SLOTS, slot.shape[1]), 0).astype(F32)
    inner = (line - place[0] * local_terms + 1).astype(F32)
    inner = jnp.where(slots == slot, inner, 0.0)
    where[...] = jnp.sum(inner, axis=1, keepdims=True).astype(jnp.int32) - 1
    total = jnp.zeros((SLOTS, design.shape[0]), F32)
    for step in range(CHUNKS):
        columns = lax.broadcasted_iota(jnp.int32, (SLOTS, chunk), 1) + step * chunk
        chosen = (columns == where[...]).astype(F32).astype(BF16)
        part(step).wait()
        total = total + lax.dot_general(
            chosen,
            held[:, step * chunk : (step + 1) * chunk],
            (((1,), (1,)), ((), ())),
            preferred_element_type=F32,
        )
    value = total.astype(BF16)
    for partner in range(devices):
        packed[partner] = value


def pack(place, picks, design, devices):
    rows = design.shape[0]
    return call(
        pack_kernel,
        "pack",
        (
            jax.ShapeDtypeStruct((devices, SLOTS, rows), BF16),
            jax.ShapeDtypeStruct((1,), jnp.int32),
            jax.ShapeDtypeStruct((SUB, picks.size), F32),
        ),
        [SCALAR, WHOLE, pl.BlockSpec(memory_space=pltpu.HBM)],
        (WHOLE, SCALAR, WHOLE),
        [
            pltpu.VMEM(design.shape, design.dtype),
            pltpu.VMEM((SLOTS, 1), jnp.int32),
            pltpu.SemaphoreType.DMA((CHUNKS,)),
        ],
    )(place, picks, design)


def unpack_kernel(target, slots, *refs):
    shape = (slots.shape[0], target.shape[1])
    lines = lax.broadcasted_iota(jnp.int32, shape, 0).astype(F32)
    moved = (lines == target[:1, :]).astype(F32).astype(BF16)
    columns = lax.dot_general(
        moved, slots[...], (((0,), (0,)), ((), ())), preferred_element_type=F32
    )
    for earlier in refs[:-1]:
        columns = columns + earlier[...].astype(F32)
    refs[-1][...] = columns.astype(BF16)


def unpack(target, slots, *earlier):
    rows = slots.shape[-1]
    operands = (target, slots.reshape(-1, rows), *earlier)
    return call(
        unpack_kernel,
        "unpack",
        jax.ShapeDtypeStruct((target.shape[1], rows), BF16),
        [WHOLE] * len(operands),
        WHOLE,
    )(*operands)


def gram_kernel(place, basis, other, sums):
    own = other.shape[0] != sums.shape[0]
    count = basis.shape[0]

    def fill(side):
        row = 0
        for top, bottom, start, stop in HALVES[side]:
            strip = lax.dot_general(
                basis[top:bottom],
                basis[start:stop],
                (((1,), (1,)), ((), ())),
                preferred_element_type=F32,
            )
            for j in range(0, stop - start, BLOCK):
                after = row + bottom - top
                piece = strip[:, j : j + BLOCK]
                sums[row:after, :] = piece if own else piece + other[row:after, :]
                row = after
        if not own:
            sums[row:, :] = other[row:, :]
            return
        resp = other.shape[0]
        inner = split_dot(other[...], basis[...], ((1,), (1,)))
        for j in range(0, count, BLOCK):
            sums[row : row + resp, :] = inner[:, j : j + BLOCK]
            row += resp
        sums[row:, :] = jnp.zeros((sums.shape[0] - row, LANES), F32)

    for side in range(2):
        pl.when(place[2] == side)(functools.partial(fill, side))


def gram(place, basis, other, half):
    count, rows = basis.shape
    return call(
        gram_kernel,
        "gram",
        jax.ShapeDtypeStruct((half, LANES), F32),
        [SCALAR, WHOLE, WHOLE],
        WHOLE,
        cost_estimate=pl.CostEstimate(
            flops=2 * count * rows * 1024,
            bytes_accessed=2 * count * rows,
            transcendentals=0,
        ),
    )(place, basis, other)


def split(value):
    parts = []
    for _ in range(3):
        parts.append(value.astype(BF16).astype(F32))
        value = value - parts[-1]
    return parts


def left_parts(value, axis):
    a, b, c = split(value)
    return jnp.concatenate([a, a, a, b, b, c], axis=axis).astype(BF16)


def right_parts(value):
    a, b, c = split(value)
    return jnp.concatenate([a, b, c, a, b, a], axis=0).astype(BF16)


def dot_parts(left, right, axis=1):
    return lax.dot_general(
        left, right, (((axis,), (0,)), ((), ())), preferred_element_type=F32
    )


def dot(left, right):
    return dot_parts(left_parts(left, 1), right_parts(right))


def split_dot(left, right, dims):
    rows = left.shape[0]
    out = lax.dot_general(
        jnp.concatenate(split(left), axis=0).astype(BF16),
        right,
        (dims, ((), ())),
        preferred_element_type=F32,
    )
    return out[2 * rows :] + out[rows : 2 * rows] + out[:rows]


def total_kernel(pieces, totals):
    total = jnp.sum(pieces[...], axis=0).astype(totals.dtype)
    totals[...] = jnp.broadcast_to(total, totals.shape)


def totals(pieces, sent):
    shape = jax.ShapeDtypeStruct(pieces.shape, sent)
    return call(total_kernel, "totals", shape, [WHOLE], WHOLE)(pieces)


def spread(piece):
    return jnp.broadcast_to(piece, (SUB, LANES))


def across(group, lane):
    index = jnp.full((SUB, LANES), lane, jnp.int32)
    return jnp.take_along_axis(group, index, axis=1, mode="promise_in_bounds")


def invert_small(columns, sub):
    for i in range(SUB):
        pivot = 1.0 / spread(columns[i][i : i + 1, :])
        column, here = columns[i], sub == i
        after = []
        for j in range(SUB):
            if j == i:
                after.append(jnp.where(here, pivot, -column * pivot))
            else:
                factor = spread(columns[j][i : i + 1, :]) * pivot
                after.append(jnp.where(here, factor, columns[j] - column * factor))
        columns = after
    return columns


def invert_block(groups):
    lane = lax.broadcasted_iota(jnp.int32, (SUB, LANES), 1)
    sub = lax.broadcasted_iota(jnp.int32, (SUB, LANES), 0)
    groups = list(groups)
    count = len(groups)
    for k in range(count):
        first = SUB * k
        mine = groups[k]
        turned = left_parts(jnp.where(lane < first, -mine, mine), 0)
        small = invert_small([across(mine, first + j) for j in range(SUB)], sub)
        inside = (lane >= first) & (lane < first + SUB)
        unit = jnp.where(lane - first == sub, 1.0, 0.0)
        mine = jnp.where(inside, unit, mine)
        terms = [small[j] * spread(mine[j : j + 1, :]) for j in range(SUB)]
        while len(terms) > 1:
            terms = [terms[i] + terms[i + 1] for i in range(0, len(terms), 2)]
        top = terms[0]
        change = dot_parts(turned, right_parts(top), 0)
        for g in range(count):
            new = jnp.where(inside, 0.0, groups[g])
            if g == k + 1:
                for j in range(SUB):
                    row = spread(top[j : j + 1, :])
                    new = new - across(groups[g], first + j) * row
            else:
                new = new - change[SUB * g : SUB * (g + 1), :]
            groups[g] = new
        groups[k] = top
    return groups


def groups_of(block):
    return [block[SUB * g : SUB * (g + 1), :] for g in range(BLOCK // SUB)]


def first_kernel(sums, inverse):
    for g, group in enumerate(invert_block(groups_of(sums[:BLOCK, :]))):
        inverse[SUB * g : SUB * (g + 1), :] = group


def first_inverse(sums):
    return call(
        first_kernel,
        "first_inverse",
        jax.ShapeDtypeStruct((BLOCK, BLOCK), F32),
        [WHOLE],
        WHOLE,
        cost_estimate=pl.CostEstimate(
            flops=2 * 10**9, bytes_accessed=10**5, transcendentals=0
        ),
    )(sums)


def finish_kernel(scale, place, *refs):
    mine, other, known_inverse, responses, basis, design, residual, pieces = refs[:8]
    work, inverse, coef = refs[8:]
    count = basis.shape[0]
    resp = responses.shape[0]
    blocks = count // BLOCK
    core = place[2]

    def place_side(side, source):
        row = 0
        for top, bottom, start, stop in HALVES[side]:
            for j in range(start, stop, BLOCK):
                after = row + bottom - top
                work[top:bottom, j : j + BLOCK] = source[row:after, :]
                row = after

    for side in range(2):
        pl.when(core == side)(functools.partial(place_side, side, mine))
        pl.when(core != side)(functools.partial(place_side, side, other))
    for i in range(blocks):
        at = pl.ds(INNER + i * resp, resp)
        tall = [mine[at, :] + other[at, :], jnp.zeros((BLOCK - resp, BLOCK), F32)]
        work[i * BLOCK : (i + 1) * BLOCK, count:] = jnp.concatenate(tall, axis=0).T

    def eliminate(k):
        start, stop = k * BLOCK, (k + 1) * BLOCK
        right = work[start:stop, stop:]
        lead = dot(inverse[...], right)
        if stop < count:
            turned = right[:, : count - stop].T
            work[stop:, stop:] = work[stop:, stop:] - dot(turned, lead)
        work[start:stop, stop:] = lead

    def step(k, carry):
        start = pl.multiple_of(k * BLOCK, BLOCK)
        groups = [
            work[pl.ds(pl.multiple_of(start + SUB * g, SUB), SUB), pl.ds(start, BLOCK)]
            for g in range(BLOCK // SUB)
        ]
        for g, group in enumerate(invert_block(groups)):
            inverse[SUB * g : SUB * (g + 1), :] = group
        for known in range(1, blocks):
            pl.when(k == known)(functools.partial(eliminate, known))
        return carry

    inverse[...] = known_inverse[...]
    eliminate(0)
    lax.fori_loop(1, blocks, step, 0)
    coef[count - BLOCK :, :] = work[count - BLOCK :, count:]
    for k in reversed(range(blocks - 1)):
        start, stop = k * BLOCK, (k + 1) * BLOCK
        coef[start:stop, :] = work[start:stop, count:] - dot(
            work[start:stop, stop:count], coef[stop:, :]
        )
    fitted = split_dot(coef[...].T[:resp, :], basis[...], ((1,), (0,)))
    left = responses[...] - fitted
    residual[...] = left
    rounded = left.astype(BF16)
    tiles = design.shape[1] // LANES
    for tile in range(0, tiles, 2):
        part = design[:, tile * LANES : (tile + 2) * LANES]
        both = jnp.dot(rounded, part, preferred_element_type=F32) * scale
        pieces[tile] = both[:, :LANES]
        pieces[tile + 1] = both[:, LANES:]
    pieces[tiles:] = jnp.zeros((pieces.shape[0] - tiles, resp, LANES), F32)


def finish(place, mine, other, inverse, responses, basis, design, pieces, scale):
    resp, rows = responses.shape
    count = basis.shape[0]
    return call(
        functools.partial(finish_kernel, scale),
        "finish",
        (
            jax.ShapeDtypeStruct((resp, rows), F32),
            jax.ShapeDtypeStruct((pieces, resp, LANES), F32),
        ),
        [SCALAR] + [WHOLE] * 6,
        (WHOLE, WHOLE),
        [
            pltpu.VMEM((count, count + LANES), F32),
            pltpu.VMEM((BLOCK, BLOCK), F32),
            pltpu.VMEM((count, LANES), F32),
        ],
    )(place, mine, other, inverse, responses, basis, design)


def summed_everywhere(pieces, axis, groups=None, sent=F32):
    return exchange(totals(exchange(pieces, axis, groups), sent), axis, groups)


def local(design, responses, picks):
    run_devices, term_devices = lax.axis_size("runs"), lax.axis_size("terms")
    resp, local_rows = responses.shape
    local_terms = design.shape[1]
    chips = run_devices // 2
    core = lax.axis_index("runs") % 2
    swap = [(i, i ^ 1) for i in range(run_devices)]
    sides = [list(range(side, run_devices, 2)) for side in range(2)]
    count = picks.size
    half = (4 + 2) * BLOCK

    def fetch(turn):
        where = jnp.stack([lax.axis_index("terms"), jnp.int32(turn), core])
        packed, most, target = pack(where, picks, design, term_devices)
        return where, target, exchange(packed, "terms"), most

    at, target, slots, most = fetch(0)
    first, slots = lax.optimization_barrier((jnp.int32(1), slots))

    def another(carry):
        turn, basis = carry
        _, lines, more, _ = fetch(turn)
        return turn + 1, unpack(lines, more, basis)

    _, basis = lax.while_loop(
        lambda carry: carry[0] * SLOTS < most[0],
        another,
        (first, unpack(target, slots)),
    )

    partner = lax.ppermute(basis, "runs", swap)
    sums = gram(at, partner, gram(at, basis, responses, half), half)

    mine = summed_everywhere(sums.reshape(chips, -1, LANES), "runs", sides)
    mine = mine.reshape(half, LANES)
    other = lax.ppermute(mine, "runs", swap)
    inverse = first_inverse(mine)

    scale = float(local_rows * run_devices) ** -0.5
    residual, pieces = finish(
        at, mine, other, inverse, responses, basis, design, run_devices, scale
    )
    gathered = summed_everywhere(pieces, "runs", sent=BF16)[: local_terms // LANES]
    correlations = gathered.transpose(1, 0, 2).reshape(resp, -1).astype(F32)
    return (residual, correlations)


def solution(mesh):
    placed = (P("runs", "terms"), P(None, "runs"), P())
    return jax.shard_map(
        local,
        mesh=mesh,
        in_specs=placed,
        out_specs=(P(None, "runs"), P(None, "terms")),
        check_vma=False,
    )
```
